128 devices in a mesh: dp: 16 (over x_hi, z, core), tensor: 8 (over x_lo, y).
Axes of the slice: x: 4 (x_hi: 2, x_lo: 2; x = x_hi * 2 + x_lo), y: 4, z: 4, core: 2. Of those that a mesh axis runs over, the one named last changes fastest.
Arguments:
- activations: bfloat16 [8192, 14336], P('dp', 'tensor'), may hold values from -6 to 6
- output_grads: bfloat16 [8192, 4096], P('dp', 'tensor'), may hold values from -6 to 6
- basis_in: float32 [16, 896, 896], P('dp'), may hold values from -0.1875 to 0.1875
- eigen_in: float32 [14336], P('dp'), may hold values from 0.1 to 1
- basis_out: float32 [4096, 512], P('tensor'), may hold values from -0.25 to 0.25
- eigen_out: float32 [4096], P('tensor'), may hold values from 0.1 to 1
Outputs:
- update: bfloat16 [14336, 4096], P(None, 'tensor')
- factor_in: float32 [896, 16, 896], P('dp', 'tensor')
- factor_out: float32 [512, 4096], P('dp', 'tensor')
The draws below stay inside these ranges and needn't reach their ends.
All inputs are finite; a program needn't handle non-finite values.
Results may differ from the reference program's by a relative error of at most 0.019.
Values may be sent and summed in bfloat16 or wider, within the bound.
A program may use at most 128 MiB of HBM per device.

```python
import math
import jax
import jax.numpy as jnp
from jax import lax

IN = 14336
OUT = 4096
BLK = 896
TOK_DEV = 512
TOKENS = 8192
BLOCKS = 16
ROWS = 512
N_DP = 16
N_TENSOR = 8


def steps_of(key, dims, shards, low, top_value):
    def one(dim, blocks):
        draws = jax.random.uniform(jax.random.fold_in(jax.random.fold_in(key, 6), dim), (blocks,), jnp.float32, low / len(shards), top_value / len(shards))
        return jnp.repeat(jnp.exp(draws), dims[dim] // blocks).reshape((-1,) + (1,) * (len(dims) - dim - 1))

    factor_of = one(*shards[0])
    for cut in shards[1:]:
        factor_of = factor_of * one(*cut)
    return factor_of


def bell_draw(rng, shape, deviation, most, cuts=(), kind=jnp.bfloat16):
    result = jax.random.normal(rng, shape, jnp.float32) * deviation
    if len(cuts) > 0:
        result = steps_of(rng, shape, cuts, -0.22, 0.18) * result
    return jnp.clip(result, min=-most, max=most).astype(kind)


def setup_inputs(seed: int = 0) -> dict:
    splits = jax.random.split(jax.random.key(seed), 7)
    return {
        "activations": bell_draw(splits[0], (TOKENS, IN), 1.0, 6.0, ((0, 16), (1, 8))),
        "output_grads": bell_draw(splits[1], (TOKENS, OUT), 1.0, 6.0, ((0, 16), (1, 8))),
        "basis_in": bell_draw(splits[2], (BLOCKS, BLK, BLK), BLK ** -0.5, 0.1875, ((0, 16),), jnp.float32),
        "eigen_in": jnp.clip(jnp.exp(math.log(1.0) - 2.3025851 * jax.random.uniform(splits[3], (IN,), jnp.float32) ** steps_of(splits[3], (IN,), ((0, 16),), -0.2, 0.2)), 0.1, 1.0),
        "basis_out": bell_draw(splits[4], (OUT, ROWS), ROWS ** -0.5, 0.25, ((0, 8),), jnp.float32),
        "eigen_out": jnp.clip(jnp.exp(math.log(1.0) - 2.3025851 * jax.random.uniform(splits[5], (OUT,), jnp.float32) ** steps_of(splits[5], (OUT,), ((0, 8),), -0.2, 0.2)), 0.1, 1.0),
    }


damping = 0.01


def reference(activations, output_grads, basis_in, eigen_in, basis_out, eigen_out):
    highest = lax.Precision.HIGHEST
    stacked_in = activations.reshape(N_DP, TOK_DEV, IN)
    stacked_out = output_grads.reshape(N_DP, TOK_DEV, OUT)

    def add_replica(total, pair):
        left, right = pair
        term = lax.dot_general(left, right, (((0,), (0,)), ((), ())), preferred_element_type=jnp.float32) / TOKENS
        rounded = lax.optimization_barrier(term.astype(jnp.bfloat16))
        return total + rounded.astype(jnp.float32), None

    grads, _ = lax.scan(add_replica, jnp.zeros((IN, OUT), jnp.float32), (stacked_in, stacked_out))

    wide_in = activations.astype(jnp.float32).reshape(TOKENS, BLOCKS, BLK)
    factor_in = jnp.einsum("tbi,tbj->ibj", wide_in, wide_in, precision=highest) / TOKENS
    wide_out = output_grads.astype(jnp.float32).reshape(TOKENS, N_TENSOR, ROWS)
    factor_out = (jnp.einsum("tsi,tsj->isj", wide_out, wide_out, precision=highest) / TOKENS).reshape(ROWS, OUT)

    blocked = grads.reshape(BLOCKS, BLK, N_TENSOR, ROWS)
    bases_out = basis_out.reshape(N_TENSOR, ROWS, ROWS)
    values_in = eigen_in.reshape(BLOCKS, BLK)
    values_out = eigen_out.reshape(N_TENSOR, ROWS)
    rotated = jnp.einsum("bij,bisk->bjsk", basis_in, blocked, precision=highest)
    rotated = jnp.einsum("bjsk,skl->bjsl", rotated, bases_out, precision=highest)
    scaled = rotated / (values_in[:, :, None, None] * values_out[None, None, :, :] + damping)
    back = jnp.einsum("bjsl,bij->bisl", scaled, basis_in, precision=highest)
    back = jnp.einsum("bisl,skl->bisk", back, bases_out, precision=highest)
    update = back.reshape(IN, OUT).astype(jnp.bfloat16)
    return update, factor_in, factor_out
```

```python
import functools
import jax
import jax.numpy as jnp
from jax import lax
from jax.experimental import pallas as pl
from jax.experimental.pallas import tpu as pltpu
from jax.sharding import PartitionSpec as P

MESH = pl.DeviceIdType.MESH
BLK = 896
ROWS = 512
TOK = 512
NP = 7
PW = 128
SCALE = 1.0 / 8192
damping = 0.01
f32, bf16 = jnp.float32, jnp.bfloat16


def where():
    dp, t = lax.axis_index("dp"), lax.axis_index("tensor")
    return dp // 8, t // 4, t % 4, (dp // 2) % 4, dp % 2


def device(xh, xl, y, z, c):
    return (xh * 8 + (z % 4) * 2 + c, xl * 4 + (y % 4))


def contract0(a, b):
    return lax.dot_general(a, b, (((0,), (0,)), ((), ())), preferred_element_type=f32)


def remote(src, dst, ssem, rsem, to):
    return pltpu.make_async_remote_copy(
        src_ref=src, dst_ref=dst, send_sem=ssem, recv_sem=rsem, device_id=to, device_id_type=MESH
    )


def greet(peers):
    barrier = pltpu.get_barrier_semaphore()
    for peer in peers:
        pl.semaphore_signal(barrier, inc=1, device_id=peer, device_id_type=MESH)
    pl.semaphore_wait(barrier, len(peers))


def grads_kernel(
    act, og, g_out, fin_out, fout_out,
    abuf, gbuf, pbuf, h1, h2, sbuf, xr, fs, fbuf, frecv, obuf, orecv,
    aloc, ad2d_s, ad2d_r, gloc, gs, gr, ys, yr, ws, wr, h1s, h1r, h2s, h2r, xs, xrs, fss, frs, oss, ors,
):
    xh, xl, y, z, c = where()
    me = xh * 8 + z * 2 + c
    mate = device(xh, xl, y, z, 1 - c)
    up, down = device(xh, xl, y + 1, z, c), device(xh, xl, y + 3, z, c)
    fore, back = device(xh, xl, y, z + 1, c), device(xh, xl, y, z + 3, c)
    beside = device(xh, 1 - xl, y, z, c)
    peers = [((me + s) % 16, xl * 4 + y) for s in range(1, 16)]
    peers += [up, down, beside, device(1 - xh, 1 - xl, y, z, c)]
    greet(peers)

    mine = pl.ds(pl.multiple_of(c * TOK, TOK), TOK)
    own_cols = pl.ds(pl.multiple_of(xl * ROWS, ROWS), ROWS)
    other_cols = pl.ds(pl.multiple_of((1 - xl) * ROWS, ROWS), ROWS)

    def cols(p):
        return pl.ds(pl.multiple_of(p * PW, PW), PW)

    def local_a(p):
        return pltpu.make_async_copy(
            act.at[:, pl.ds(pl.multiple_of(c * BLK + p * PW, PW), PW)], abuf.at[0, mine, cols(p)], aloc.at[p])

    def mate_a(p):
        return remote(
            act.at[:, pl.ds(pl.multiple_of((1 - c) * BLK + p * PW, PW), PW)], abuf.at[0, mine, cols(p)],
            ad2d_s.at[p], ad2d_r.at[p], mate)

    for p in range(NP):
        mate_a(p).start()
        local_a(p).start()
    g_local = pltpu.make_async_copy(og, gbuf.at[mine, own_cols], gloc)
    g_beside = remote(og, gbuf.at[mine, own_cols], gs.at[0], gr.at[0], beside)
    g_mate = remote(og, gbuf.at[mine, own_cols], gs.at[1], gr.at[1], mate)
    g_pass = remote(gbuf.at[mine, other_cols], gbuf.at[mine, other_cols], gs.at[2], gr.at[2], mate)
    g_local.start()
    g_beside.start()
    g_mate.start()

    def send_up(p):
        return remote(abuf.at[0, :, cols(p)], abuf.at[3, :, cols(p)], ys.at[0, p], yr.at[0, p], up)

    def send_down(p):
        return remote(abuf.at[0, :, cols(p)], abuf.at[1, :, cols(p)], ys.at[1, p], yr.at[1, p], down)

    def pass_down(p):
        return remote(
            abuf.at[1, 0:TOK, cols(p)], abuf.at[2, 0:TOK, cols(p)], ws.at[0, p], wr.at[0, p], down)

    def pass_up(p):
        return remote(
            abuf.at[3, TOK : 2 * TOK, cols(p)], abuf.at[2, TOK : 2 * TOK, cols(p)], ws.at[1, p], wr.at[1, p], up)

    def ready(p):
        local_a(p).wait()
        mate_a(p).wait_recv()

    for p in range(NP):
        ready(p)
        if p < 2:
            send_up(p).start()
            send_down(p).start()

    def factor_rows(p, carry):
        fs[cols(p), :] = contract0(abuf[0, :, cols(p)], abuf[0])
        return carry

    lax.fori_loop(0, NP, factor_rows, 0)
    fbuf[:, 48:64, :] = jnp.zeros((16, 16, BLK), bf16)

    def strips(r, carry):
        fbuf[r, 0:56, :] = fs[pl.ds(pl.multiple_of(r * 56, 8), 56), :].astype(bf16)
        return carry

    lax.fori_loop(0, 16, strips, 0)
    g_local.wait()
    g_here = gbuf[mine, own_cols]
    obuf[...] = contract0(g_here, g_here).astype(bf16)

    def send_factor(s):
        r = (me + s) % 16
        return (
            remote(fbuf.at[r], frecv.at[s], fss.at[s], frs.at[s], (r, xl * 4 + y)),
            remote(obuf.at[pl.ds(pl.multiple_of(r * 32, 32), 32), :], orecv.at[s], oss.at[s], ors.at[s],
                   (r, xl * 4 + y)),
        )

    def start_factor(s, carry):
        for copy in send_factor(s):
            copy.start()
        return carry

    lax.fori_loop(1, 16, start_factor, 0)
    g_beside.wait_recv()
    g_pass.start()
    g_mate.wait_recv()
    g_pass.wait_recv()

    def partial(d, p):
        e = (y - z + d + 4) % 4
        a = abuf[d, :, cols(p)]
        for tx in range(2):
            pbuf[e, tx, cols(p), :] = contract0(a, gbuf[:, tx * ROWS : (tx + 1) * ROWS]).astype(bf16)

    def hop1(p):
        return (
            remote(pbuf.at[2, 0, cols(p), :], h1.at[0, cols(p), :], h1s.at[0, p], h1r.at[0, p], fore),
            remote(pbuf.at[2, 1, cols(p), :], h1.at[1, cols(p), :], h1s.at[1, p], h1r.at[1, p], back),
        )

    def hop2(p):
        return (
            remote(pbuf.at[1, :, cols(p), :], h2.at[0, :, cols(p), :], h2s.at[0, p], h2r.at[0, p], fore),
            remote(pbuf.at[3, :, cols(p), :], h2.at[1, :, cols(p), :], h2s.at[1, p], h2r.at[1, p], back),
        )

    def to_owner(tx, p):
        return remote(
            sbuf.at[tx, cols(p), :], xr.at[xh, cols(p), :], xs.at[tx, p], xrs.at[xh, p], device(xl, tx, y, z, c))

    def from_half(kx, p):
        return remote(
            sbuf.at[0, cols(p), :], xr.at[kx, cols(p), :], xs.at[0, p], xrs.at[kx, p], beside)

    def is_self(tx):
        return jnp.logical_and(xh == xl, xl == tx)

    def comes_from_self(kx):
        return jnp.logical_and(xh == xl, kx == xh)

    def step(i, carry):
        @pl.when(jnp.logical_and(i >= 2, i < NP + 2))
        def _():
            p = i - 2
            for copy in hop1(p):
                copy.wait_recv()
            pbuf[1, 0, cols(p), :] = (
                pbuf[1, 0, cols(p), :].astype(f32) + h1[0, cols(p), :].astype(f32)).astype(bf16)
            pbuf[3, 1, cols(p), :] = (
                pbuf[3, 1, cols(p), :].astype(f32) + h1[1, cols(p), :].astype(f32)).astype(bf16)
            for copy in hop2(p):
                copy.start()

        @pl.when(i < NP)
        def _():
            @pl.when(i + 2 < NP)
            def _():
                send_up(i).wait_send()
                send_down(i).wait_send()
                send_up(i + 2).start()
                send_down(i + 2).start()

            partial(0, i)
            send_down(i).wait_recv()
            pass_down(i).start()
            send_up(i).wait_recv()
            pass_up(i).start()
            partial(1, i)
            partial(3, i)

        @pl.when(jnp.logical_and(i >= 1, i < NP + 1))
        def _():
            p = i - 1
            pass_down(p).wait_recv()
            pass_up(p).wait_recv()
            partial(2, p)
            for copy in hop1(p):
                copy.start()

        @pl.when(jnp.logical_and(i >= 3, i < NP + 3))
        def _():
            p = i - 3
            for copy in hop2(p):
                copy.wait_recv()
            for tx in range(2):
                total = (pbuf[0, tx, cols(p), :].astype(f32) + h2[0, tx, cols(p), :].astype(f32)
                         + h2[1, tx, cols(p), :].astype(f32))
                sbuf[tx, cols(p), :] = total.astype(bf16)

                @pl.when(is_self(tx))
                def _():
                    xr[xh, cols(p), :] = total.astype(bf16)

                @pl.when(jnp.logical_not(is_self(tx)))
                def _():
                    to_owner(tx, p).start()

        @pl.when(i >= 4)
        def _():
            p = i - 4
            for kx in range(2):
                @pl.when(jnp.logical_not(comes_from_self(kx)))
                def _():
                    from_half(kx, p).wait_recv()
            g_out[cols(p), :] = (xr[0, cols(p), :].astype(f32) + xr[1, cols(p), :].astype(f32)) * SCALE

        return carry

    lax.fori_loop(0, NP + 4, step, 0)

    def take(s, carry):
        for copy in send_factor(s):
            copy.wait_recv()
        return carry

    lax.fori_loop(1, 16, take, 0)
    here = fbuf[me, 0:56, :].astype(f32)
    there = frecv[1, 0:56, :].astype(f32)
    for s in range(2, 16):
        term = frecv[s, 0:56, :].astype(f32)
        if s % 2 == 0:
            here += term
        else:
            there += term
    fin_out[c] = here * SCALE
    fin_out[1 - c] = there * SCALE
    total = obuf[pl.ds(pl.multiple_of(me * 32, 32), 32), :].astype(f32)
    for s in range(1, 16):
        total += orecv[s].astype(f32)
    fout_out[...] = total * SCALE

    for copy in (g_beside, g_mate, g_pass):
        copy.wait_send()

    def finish(p, carry):
        mate_a(p).wait_send()
        for copy in (pass_down(p), pass_up(p)) + hop1(p) + hop2(p):
            copy.wait_send()
        for tx in range(2):
            @pl.when(jnp.logical_not(is_self(tx)))
            def _():
                to_owner(tx, p).wait_send()
        return carry

    lax.fori_loop(0, NP, finish, 0)
    for p in range(NP - 2, NP):
        send_up(p).wait_send()
        send_down(p).wait_send()

    def finish_factor(s, carry):
        for copy in send_factor(s):
            copy.wait_send()
        return carry

    lax.fori_loop(1, 16, finish_factor, 0)


def weight_grads(activations, output_grads):
    dma = pltpu.SemaphoreType.DMA
    any_spec = pl.BlockSpec(memory_space=pl.ANY)
    vmem = pl.BlockSpec(memory_space=pltpu.VMEM)
    return pl.pallas_call(
        grads_kernel,
        out_shape=(
            jax.ShapeDtypeStruct((BLK, ROWS), f32),
            jax.ShapeDtypeStruct((2, 56, BLK), f32),
            jax.ShapeDtypeStruct((32, ROWS), f32),
        ),
        in_specs=[any_spec, any_spec],
        out_specs=(vmem, vmem, vmem),
        scratch_shapes=[
            pltpu.VMEM((4, 2 * TOK, BLK), bf16),
            pltpu.VMEM((2 * TOK, 2 * ROWS), bf16),
            pltpu.VMEM((4, 2, BLK, ROWS), bf16),
            pltpu.VMEM((2, BLK, ROWS), bf16),
            pltpu.VMEM((2, 2, BLK, ROWS), bf16),
            pltpu.VMEM((2, BLK, ROWS), bf16),
            pltpu.VMEM((2, BLK, ROWS), bf16),
            pltpu.VMEM((BLK, BLK), f32),
            pltpu.VMEM((16, 64, BLK), bf16),
            pltpu.VMEM((16, 64, BLK), bf16),
            pltpu.VMEM((ROWS, ROWS), bf16),
            pltpu.VMEM((16, 32, ROWS), bf16),
            dma((NP,)), dma((NP,)), dma((NP,)),
            dma, dma((3,)), dma((3,)),
            dma((2, NP)), dma((2, NP)), dma((2, NP)), dma((2, NP)),
            dma((2, NP)), dma((2, NP)), dma((2, NP)), dma((2, NP)),
            dma((2, NP)), dma((2, NP)),
            dma((16,)), dma((16,)), dma((16,)), dma((16,)),
        ],
        compiler_params=pltpu.CompilerParams(
            collective_id=0, has_side_effects=True, vmem_limit_bytes=52 * 2**20),
        cost_estimate=pl.CostEstimate(flops=9_500_000_000, bytes_accessed=6_000_000, transcendentals=0),
        name="weight_grads",
    )(activations, output_grads)


def body(activations, output_grads, basis_in, eigen_in, basis_out, eigen_out):
    highest = lax.Precision.HIGHEST
    grad, fin, factor_out = weight_grads(activations, output_grads)
    factor_in = jnp.transpose(fin, (1, 0, 2))
    grad = grad[None]
    values_in = eigen_in.reshape(1, BLK)
    rotated = jnp.einsum("bij,bik->bjk", basis_in, grad, precision=highest)
    rotated = jnp.einsum("bjk,kl->bjl", rotated, basis_out, precision=highest)
    scaled = rotated / (values_in[:, :, None] * eigen_out[None, None, :] + damping)
    back = jnp.einsum("bjl,bij->bil", scaled, basis_in, precision=highest)
    back = jnp.einsum("bil,kl->bik", back, basis_out, precision=highest)
    worker_slab = back.reshape(BLK, ROWS).astype(jnp.bfloat16)
    update = lax.all_gather(worker_slab, "dp", axis=0, tiled=True)
    return (update, factor_in, factor_out)


def solution(mesh):
    in_specs = (
        P("dp", "tensor"),
        P("dp", "tensor"),
        P("dp", None, None),
        P("dp"),
        P("tensor", None),
        P("tensor"),
    )
    out_specs = (P(None, "tensor"), P("dp", "tensor", None), P("dp", "tensor"))
    return jax.shard_map(body, mesh=mesh, in_specs=in_specs, out_specs=out_specs, check_vma=False)
```

```python
import functools
import jax
import jax.numpy as jnp
from jax import lax
from jax.experimental import pallas as pl
from jax.experimental.pallas import tpu as pltpu
from jax.sharding import PartitionSpec as P

MESH = pl.DeviceIdType.MESH
BLK = 896
ROWS = 512
TOK = 512
NP = 7
PW = 128
SCALE = 1.0 / 8192
damping = 0.01
f32, bf16 = jnp.float32, jnp.bfloat16


def where():
    dp, t = lax.axis_index("dp"), lax.axis_index("tensor")
    return dp // 8, t // 4, t % 4, (dp // 2) % 4, dp % 2


def device(xh, xl, y, z, c):
    return (xh * 8 + (z % 4) * 2 + c, xl * 4 + (y % 4))


def contract0(a, b):
    return lax.dot_general(a, b, (((0,), (0,)), ((), ())), preferred_element_type=f32)


def remote(src, dst, ssem, rsem, to):
    return pltpu.make_async_remote_copy(
        src_ref=src, dst_ref=dst, send_sem=ssem, recv_sem=rsem, device_id=to, device_id_type=MESH
    )


def greet(peers):
    barrier = pltpu.get_barrier_semaphore()
    for peer in peers:
        pl.semaphore_signal(barrier, inc=1, device_id=peer, device_id_type=MESH)
    pl.semaphore_wait(barrier, len(peers))


def grads_kernel(
    act, og, g_out, fin_out, fout_out,
    abuf, gbuf, pbuf, h1, h2, sbuf, xr, fs, fbuf, frecv, obuf, orecv,
    aloc, ad2d_s, ad2d_r, gloc, gs, gr, ys, yr, ws, wr, h1s, h1r, h2s, h2r, xs, xrs, fss, frs, oss, ors,
):
    xh, xl, y, z, c = where()
    me = xh * 8 + z * 2 + c
    mate = device(xh, xl, y, z, 1 - c)
    up, down = device(xh, xl, y + 1, z, c), device(xh, xl, y + 3, z, c)
    fore, back = device(xh, xl, y, z + 1, c), device(xh, xl, y, z + 3, c)
    beside = device(xh, 1 - xl, y, z, c)
    peers = [((me + s) % 16, xl * 4 + y) for s in range(1, 16)]
    peers += [up, down, beside, device(1 - xh, 1 - xl, y, z, c)]
    greet(peers)

    mine = pl.ds(pl.multiple_of(c * TOK, TOK), TOK)
    own_cols = pl.ds(pl.multiple_of(xl * ROWS, ROWS), ROWS)
    other_cols = pl.ds(pl.multiple_of((1 - xl) * ROWS, ROWS), ROWS)

    def cols(p):
        return pl.ds(pl.multiple_of(p * PW, PW), PW)

    def local_a(p):
        return pltpu.make_async_copy(
            act.at[:, pl.ds(pl.multiple_of(c * BLK + p * PW, PW), PW)], abuf.at[0, mine, cols(p)], aloc.at[p])

    def mate_a(p):
        return remote(
            act.at[:, pl.ds(pl.multiple_of((1 - c) * BLK + p * PW, PW), PW)], abuf.at[0, mine, cols(p)],
            ad2d_s.at[p], ad2d_r.at[p], mate)

    for p in range(NP):
        mate_a(p).start()
        local_a(p).start()
    g_local = pltpu.make_async_copy(og, gbuf.at[mine, own_cols], gloc)
    g_beside = remote(og, gbuf.at[mine, own_cols], gs.at[0], gr.at[0], beside)
    g_mate = remote(og, gbuf.at[mine, own_cols], gs.at[1], gr.at[1], mate)
    g_pass = remote(gbuf.at[mine, other_cols], gbuf.at[mine, other_cols], gs.at[2], gr.at[2], mate)
    g_local.start()
    g_beside.start()
    g_mate.start()

    def send_up(p):
        return remote(abuf.at[0, :, cols(p)], abuf.at[3, :, cols(p)], ys.at[0, p], yr.at[0, p], up)

    def send_down(p):
        return remote(abuf.at[0, :, cols(p)], abuf.at[1, :, cols(p)], ys.at[1, p], yr.at[1, p], down)

    def pass_down(p):
        return remote(
            abuf.at[1, 0:TOK, cols(p)], abuf.at[2, 0:TOK, cols(p)], ws.at[0, p], wr.at[0, p], down)

    def pass_up(p):
        return remote(
            abuf.at[3, TOK : 2 * TOK, cols(p)], abuf.at[2, TOK : 2 * TOK, cols(p)], ws.at[1, p], wr.at[1, p], up)

    def ready(p):
        local_a(p).wait()
        mate_a(p).wait_recv()

    for p in range(NP):
        ready(p)
        if p < 2:
            send_up(p).start()
            send_down(p).start()

    def factor_rows(p, carry):
        fs[cols(p), :] = contract0(abuf[0, :, cols(p)], abuf[0])
        return carry

    lax.fori_loop(0, NP, factor_rows, 0)
    fbuf[:, 48:64, :] = jnp.zeros((16, 16, BLK), bf16)

    def strips(r, carry):
        fbuf[r, 0:56, :] = fs[pl.ds(pl.multiple_of(r * 56, 8), 56), :].astype(bf16)
        return carry

    lax.fori_loop(0, 16, strips, 0)
    g_local.wait()
    g_here = gbuf[mine, own_cols]
    obuf[...] = contract0(g_here, g_here).astype(bf16)

    def send_factor(s):
        r = (me + s) % 16
        return (
            remote(fbuf.at[r], frecv.at[s], fss.at[s], frs.at[s], (r, xl * 4 + y)),
            remote(obuf.at[pl.ds(pl.multiple_of(r * 32, 32), 32), :], orecv.at[s], oss.at[s], ors.at[s],
                   (r, xl * 4 + y)),
        )

    def start_factor(s, carry):
        for copy in send_factor(s):
            copy.start()
        return carry

    lax.fori_loop(1, 16, start_factor, 0)
    g_beside.wait_recv()
    g_pass.start()
    g_mate.wait_recv()
    g_pass.wait_recv()

    def partial(d, p):
        e = (y - z + d + 4) % 4
        a = abuf[d, :, cols(p)]
        for tx in range(2):
            pbuf[e, tx, cols(p), :] = contract0(a, gbuf[:, tx * ROWS : (tx + 1) * ROWS]).astype(bf16)

    def hop1(p):
        return (
            remote(pbuf.at[2, 0, cols(p), :], h1.at[0, cols(p), :], h1s.at[0, p], h1r.at[0, p], fore),
            remote(pbuf.at[2, 1, cols(p), :], h1.at[1, cols(p), :], h1s.at[1, p], h1r.at[1, p], back),
        )

    def hop2(p):
        return (
            remote(pbuf.at[1, :, cols(p), :], h2.at[0, :, cols(p), :], h2s.at[0, p], h2r.at[0, p], fore),
            remote(pbuf.at[3, :, cols(p), :], h2.at[1, :, cols(p), :], h2s.at[1, p], h2r.at[1, p], back),
        )

    def to_owner(tx, p):
        return remote(
            sbuf.at[tx, cols(p), :], xr.at[xh, cols(p), :], xs.at[tx, p], xrs.at[xh, p], device(xl, tx, y, z, c))

    def from_half(kx, p):
        return remote(
            sbuf.at[0, cols(p), :], xr.at[kx, cols(p), :], xs.at[0, p], xrs.at[kx, p], beside)

    def is_self(tx):
        return jnp.logical_and(xh == xl, xl == tx)

    def comes_from_self(kx):
        return jnp.logical_and(xh == xl, kx == xh)

    def step(i, carry):
        @pl.when(jnp.logical_and(i >= 2, i < NP + 2))
        def _():
            p = i - 2
            for copy in hop1(p):
                copy.wait_recv()
            pbuf[1, 0, cols(p), :] = (
                pbuf[1, 0, cols(p), :].astype(f32) + h1[0, cols(p), :].astype(f32)).astype(bf16)
            pbuf[3, 1, cols(p), :] = (
                pbuf[3, 1, cols(p), :].astype(f32) + h1[1, cols(p), :].astype(f32)).astype(bf16)
            for copy in hop2(p):
                copy.start()

        @pl.when(i < NP)
        def _():
            @pl.when(i + 2 < NP)
            def _():
                send_up(i).wait_send()
                send_down(i).wait_send()
                send_up(i + 2).start()
                send_down(i + 2).start()

            partial(0, i)
            send_down(i).wait_recv()
            pass_down(i).start()
            send_up(i).wait_recv()
            pass_up(i).start()
            partial(1, i)
            partial(3, i)

        @pl.when(jnp.logical_and(i >= 1, i < NP + 1))
        def _():
            p = i - 1
            pass_down(p).wait_recv()
            pass_up(p).wait_recv()
            partial(2, p)
            for copy in hop1(p):
                copy.start()

        @pl.when(jnp.logical_and(i >= 3, i < NP + 3))
        def _():
            p = i - 3
            for copy in hop2(p):
                copy.wait_recv()
            for tx in range(2):
                total = (pbuf[0, tx, cols(p), :].astype(f32) + h2[0, tx, cols(p), :].astype(f32)
                         + h2[1, tx, cols(p), :].astype(f32))
                sbuf[tx, cols(p), :] = total.astype(bf16)

                @pl.when(is_self(tx))
                def _():
                    xr[xh, cols(p), :] = total.astype(bf16)

                @pl.when(jnp.logical_not(is_self(tx)))
                def _():
                    to_owner(tx, p).start()

        @pl.when(i >= 4)
        def _():
            p = i - 4
            for kx in range(2):
                @pl.when(jnp.logical_not(comes_from_self(kx)))
                def _():
                    from_half(kx, p).wait_recv()
            g_out[cols(p), :] = (xr[0, cols(p), :].astype(f32) + xr[1, cols(p), :].astype(f32)) * SCALE

        return carry

    lax.fori_loop(0, NP + 4, step, 0)

    def take(s, carry):
        for copy in send_factor(s):
            copy.wait_recv()
        return carry

    lax.fori_loop(1, 16, take, 0)
    here = fbuf[me, 0:56, :].astype(f32)
    there = frecv[1, 0:56, :].astype(f32)
    for s in range(2, 16):
        term = frecv[s, 0:56, :].astype(f32)
        if s % 2 == 0:
            here += term
        else:
            there += term
    fin_out[c] = here * SCALE
    fin_out[1 - c] = there * SCALE
    total = obuf[pl.ds(pl.multiple_of(me * 32, 32), 32), :].astype(f32)
    for s in range(1, 16):
        total += orecv[s].astype(f32)
    fout_out[...] = total * SCALE

    for copy in (g_beside, g_mate, g_pass):
        copy.wait_send()

    def finish(p, carry):
        mate_a(p).wait_send()
        for copy in (pass_down(p), pass_up(p)) + hop1(p) + hop2(p):
            copy.wait_send()
        for tx in range(2):
            @pl.when(jnp.logical_not(is_self(tx)))
            def _():
                to_owner(tx, p).wait_send()
        return carry

    lax.fori_loop(0, NP, finish, 0)
    for p in range(NP - 2, NP):
        send_up(p).wait_send()
        send_down(p).wait_send()

    def finish_factor(s, carry):
        for copy in send_factor(s):
            copy.wait_send()
        return carry

    lax.fori_loop(1, 16, finish_factor, 0)


def weight_grads(activations, output_grads):
    dma = pltpu.SemaphoreType.DMA
    any_spec = pl.BlockSpec(memory_space=pl.ANY)
    vmem = pl.BlockSpec(memory_space=pltpu.VMEM)
    return pl.pallas_call(
        grads_kernel,
        out_shape=(
            jax.ShapeDtypeStruct((BLK, ROWS), f32),
            jax.ShapeDtypeStruct((2, 56, BLK), f32),
            jax.ShapeDtypeStruct((32, ROWS), f32),
        ),
        in_specs=[any_spec, any_spec],
        out_specs=(vmem, vmem, vmem),
        scratch_shapes=[
            pltpu.VMEM((4, 2 * TOK, BLK), bf16),
            pltpu.VMEM((2 * TOK, 2 * ROWS), bf16),
            pltpu.VMEM((4, 2, BLK, ROWS), bf16),
            pltpu.VMEM((2, BLK, ROWS), bf16),
            pltpu.VMEM((2, 2, BLK, ROWS), bf16),
            pltpu.VMEM((2, BLK, ROWS), bf16),
            pltpu.VMEM((2, BLK, ROWS), bf16),
            pltpu.VMEM((BLK, BLK), f32),
            pltpu.VMEM((16, 64, BLK), bf16),
            pltpu.VMEM((16, 64, BLK), bf16),
            pltpu.VMEM((ROWS, ROWS), bf16),
            pltpu.VMEM((16, 32, ROWS), bf16),
            dma((NP,)), dma((NP,)), dma((NP,)),
            dma, dma((3,)), dma((3,)),
            dma((2, NP)), dma((2, NP)), dma((2, NP)), dma((2, NP)),
            dma((2, NP)), dma((2, NP)), dma((2, NP)), dma((2, NP)),
            dma((2, NP)), dma((2, NP)),
            dma((16,)), dma((16,)), dma((16,)), dma((16,)),
        ],
        compiler_params=pltpu.CompilerParams(
            collective_id=0, has_side_effects=True, vmem_limit_bytes=52 * 2**20),
        cost_estimate=pl.CostEstimate(flops=9_500_000_000, bytes_accessed=6_000_000, transcendentals=0),
        name="weight_grads",
    )(activations, output_grads)


def split(x):
    high = x.astype(bf16)
    return high, (x - high.astype(f32)).astype(bf16)


def dot(a, b):
    return jnp.dot(a, b, preferred_element_type=f32)


PARTS = ((0, 256), (256, 256), (512, 192), (704, 192))
FIRST = (0, 512)
LAST = (512, 384)


def update_kernel(
    g, basis_in, eigen_in, basis_out, eigen_out, u,
    qh, ql, vbuf,
    zs, zr, fs, fr, xs, xr, ds, dr,
):
    xh, xl, y, z, c = where()
    me = xh * 8 + z * 2 + c
    mate = device(xh, xl, y, z, 1 - c)
    fore, back = device(xh, xl, y, z + 1, c), device(xh, xl, y, z + 3, c)
    across = device(1 - xh, xl, y, z, c)
    greet([mate, fore, back, across])

    for p in range(NP):
        high, low = split(basis_in[0, p * PW : (p + 1) * PW, :])
        qh[p * PW : (p + 1) * PW, :] = high
        ql[p * PW : (p + 1) * PW, :] = low
    gh, gl = split(g[...])
    oh, ol = split(basis_out[...])
    for start, size in (FIRST, LAST):
        rows = slice(start, start + size)
        mid = contract0(qh[:, rows], gh) + contract0(qh[:, rows], gl) + contract0(ql[:, rows], gh)
        mh, ml = split(mid)
        turned = dot(mh, oh) + dot(mh, ol) + dot(ml, oh)
        column = jnp.transpose(jnp.broadcast_to(eigen_in[:, rows], (128, size)))
        for k in range(ROWS // 128):
            lanes = slice(k * 128, (k + 1) * 128)
            scaled = turned[:, lanes] / (column * eigen_out[:, lanes] + damping)
            vbuf[rows, lanes] = scaled.astype(bf16)
        back_out = lax.dot_general(
            vbuf[rows, :], oh, (((1,), (1,)), ((), ())), preferred_element_type=f32)
        vbuf[rows, :] = back_out.astype(bf16)

    def part(other, dz, core, start, size):
        half = (1 - xh) if other else xh
        base = (half * 8 + ((z + dz) % 4) * 2 + core) * BLK
        return u.at[pl.ds(pl.multiple_of(base + start, 64), size), :]

    def copy(other, dz, start, size, ssem, rsem, to):
        return remote(part(other, dz, c, start, size), part(other, dz, c, start, size), ssem, rsem, to)

    waits = []

    def go(descriptor):
        descriptor.start()
        waits.append(descriptor)
        return descriptor

    def ring(sem, other, start, size):
        go(copy(other, 0, start, size, zs.at[0, sem], zr.at[0, sem], fore))
        go(copy(other, 0, start, size, zs.at[1, sem], zr.at[1, sem], back))

    def ring_take(sem, other, start, size):
        copy(other, 3, start, size, zs.at[0, sem], zr.at[0, sem], fore).wait_recv()
        copy(other, 1, start, size, zs.at[1, sem], zr.at[1, sem], back).wait_recv()

    def relay(sem, other, start, size):
        half = size // 2
        go(copy(other, 3, start, half, fs.at[0, sem], fr.at[0, sem], fore))
        go(copy(other, 1, start + half, half, fs.at[1, sem], fr.at[1, sem], back))

    def relay_take(sem, other, start, size):
        half = size // 2
        copy(other, 2, start, half, fs.at[0, sem], fr.at[0, sem], fore).wait_recv()
        copy(other, 2, start + half, half, fs.at[1, sem], fr.at[1, sem], back).wait_recv()

    def cross(sem, dz, start, size):
        go(copy(False, dz, start, size, xs.at[sem], xr.at[sem], across))

    def cross_take(sem, dz, start, size):
        copy(True, dz, start, size, xs.at[sem], xr.at[sem], across).wait_recv()

    given = []

    def share(other, dz, start, size):
        sem = len(given)
        go(copy(other, dz, start, size, ds.at[sem], dr.at[sem], mate))
        given.append((other, dz, start, size))

    for k, (start, size) in enumerate(PARTS):
        block = dot(qh[start : start + size, :], vbuf[...]).astype(bf16)
        u[pl.ds(pl.multiple_of(me * BLK + start, 64), size), :] = block
        if k < 2:
            cross(k, 0, start, size)
            ring(k, False, start, size)
        if k == 3:
            ring(2, False, *LAST)
            cross(2, 0, *LAST)
    share(False, 0, *FIRST)
    share(False, 0, *LAST)
    for k in range(2):
        ring_take(k, False, *PARTS[k])
        relay(k, False, *PARTS[k])
    for k in range(2):
        cross_take(k, 0, *PARTS[k])
        ring(3 + k, True, *PARTS[k])
    ring_take(2, False, *LAST)
    relay(2, False, *LAST)
    cross(3, 1, *LAST)
    cross(4, 3, *LAST)
    for dz in (1, 3):
        share(False, dz, 0, BLK)
    share(True, 0, *FIRST)
    for k in range(2):
        relay_take(k, False, *PARTS[k])
    share(False, 2, *FIRST)
    relay_take(2, False, *LAST)
    cross(5, 2, *LAST)
    share(False, 2, *LAST)
    cross_take(2, 0, *LAST)
    share(True, 0, *LAST)
    for k in range(2):
        ring_take(3 + k, True, *PARTS[k])
        relay(3 + k, True, *PARTS[k])
    share(True, 1, *FIRST)
    share(True, 3, *FIRST)
    cross_take(3, 1, *LAST)
    share(True, 1, *LAST)
    cross_take(4, 3, *LAST)
    share(True, 3, *LAST)
    cross_take(5, 2, *LAST)
    share(True, 2, *LAST)
    for k in range(2):
        relay_take(3 + k, True, *PARTS[k])
        share(True, 2, *PARTS[k])
    for sem, (other, dz, start, size) in enumerate(given):
        ref = part(other, dz, 1 - c, start, size)
        remote(ref, ref, ds.at[sem], dr.at[sem], mate).wait_recv()
    for descriptor in waits:
        descriptor.wait_send()


def rotate_and_gather(grad, basis_in, eigen_in, basis_out, eigen_out):
    dma = pltpu.SemaphoreType.DMA
    vmem = pl.BlockSpec(memory_space=pltpu.VMEM)
    return pl.pallas_call(
        update_kernel,
        out_shape=pltpu.VMEM((16 * BLK, ROWS), bf16),
        in_specs=[vmem] * 5,
        out_specs=vmem,
        scratch_shapes=[
            pltpu.VMEM((BLK, BLK), bf16),
            pltpu.VMEM((BLK, BLK), bf16),
            pltpu.VMEM((BLK, ROWS), bf16),
            dma((2, 5)), dma((2, 5)), dma((2, 5)), dma((2, 5)),
            dma((6,)), dma((6,)), dma((20,)), dma((20,)),
        ],
        compiler_params=pltpu.CompilerParams(
            collective_id=1, has_side_effects=True, vmem_limit_bytes=36 * 2**20),
        cost_estimate=pl.CostEstimate(flops=5_000_000_000, bytes_accessed=20_000_000, transcendentals=0),
        name="rotate_and_gather",
    )(grad, basis_in, eigen_in, basis_out, eigen_out)


def body(activations, output_grads, basis_in, eigen_in, basis_out, eigen_out):
    grad, fin, factor_out = weight_grads(activations, output_grads)
    factor_in = jnp.transpose(fin, (1, 0, 2))
    update = rotate_and_gather(grad, basis_in, eigen_in.reshape(1, BLK), basis_out, eigen_out.reshape(1, ROWS))
    return (update, factor_in, factor_out)


def solution(mesh):
    in_specs = (
        P("dp", "tensor"),
        P("dp", "tensor"),
        P("dp", None, None),
        P("dp"),
        P("tensor", None),
        P("tensor"),
    )
    out_specs = (P(None, "tensor"), P("dp", "tensor", None), P("dp", "tensor"))
    return jax.shard_map(body, mesh=mesh, in_specs=in_specs, out_specs=out_specs, check_vma=False)
```

```python
import functools
import jax
import jax.numpy as jnp
from jax import lax
from jax.experimental import pallas as pl
from jax.experimental.pallas import tpu as pltpu
from jax.sharding import PartitionSpec as P

MESH = pl.DeviceIdType.MESH
BLK = 896
ROWS = 512
TOK = 512
NP = 7
PW = 128
SCALE = 1.0 / 8192
LAG2, LAG3, LAG4 = 2, 3, 4
STRIPS = NP + 1
damping = 0.01
f32, bf16 = jnp.float32, jnp.bfloat16


def where():
    dp, t = lax.axis_index("dp"), lax.axis_index("tensor")
    return dp // 8, t // 4, t % 4, (dp // 2) % 4, dp % 2


def device(xh, xl, y, z, c):
    return (xh * 8 + (z % 4) * 2 + c, xl * 4 + (y % 4))


def contract0(a, b):
    return lax.dot_general(a, b, (((0,), (0,)), ((), ())), preferred_element_type=f32)


def remote(src, dst, ssem, rsem, to):
    return pltpu.make_async_remote_copy(
        src_ref=src, dst_ref=dst, send_sem=ssem, recv_sem=rsem, device_id=to, device_id_type=MESH
    )


def greet(peers):
    barrier = pltpu.get_barrier_semaphore()
    for peer in peers:
        pl.semaphore_signal(barrier, inc=1, device_id=peer, device_id_type=MESH)
    pl.semaphore_wait(barrier, len(peers))


def split(x):
    high = x.astype(bf16)
    return high, (x - high.astype(f32)).astype(bf16)


def dot(a, b):
    return jnp.dot(a, b, preferred_element_type=f32)


PARTS = ((0, 256), (256, 256), (512, 192), (704, 192))
FIRST = (0, 512)
LAST = (512, 384)


def step_kernel(
    act, og, basis_in, eigen_in, basis_out, eigen_out, u, fin_out, fout_out,
    abuf, gbuf, pbuf, h1, h2, sbuf, xr, fs, fbuf, fswap, frecv, obuf, oswap, orecv,
    aloc, ad2d_s, ad2d_r, gloc, gs, gr, ys, yr, ws, wr, h1s, h1r, h2s, h2r, xs, xrs, fss, frs, oss, ors,
    qh, ql, r1, vbuf, qloc, zs, zr, vs, vr, cs, cr, ds, dr,
):
    xh, xl, y, z, c = where()
    me = xh * 8 + z * 2 + c
    mate = device(xh, xl, y, z, 1 - c)
    up, down = device(xh, xl, y + 1, z, c), device(xh, xl, y + 3, z, c)
    fore, back = device(xh, xl, y, z + 1, c), device(xh, xl, y, z + 3, c)
    beside = device(xh, 1 - xl, y, z, c)
    across = device(1 - xh, xl, y, z, c)
    column = [(dz, cc) for cc in range(2) for dz in range(4)][1:]
    peers = [device(xh, xl, y, z + dz, (c + cc) % 2) for dz, cc in column]
    greet(peers + [up, down, beside, across, device(1 - xh, 1 - xl, y, z, c)])

    mine = pl.ds(pl.multiple_of(c * TOK, TOK), TOK)
    own_cols = pl.ds(pl.multiple_of(xl * ROWS, ROWS), ROWS)
    other_cols = pl.ds(pl.multiple_of((1 - xl) * ROWS, ROWS), ROWS)

    def cols(p):
        return pl.ds(pl.multiple_of(p * PW, PW), PW)

    def local_a(p):
        return pltpu.make_async_copy(
            act.at[:, pl.ds(pl.multiple_of(c * BLK + p * PW, PW), PW)], abuf.at[0, mine, cols(p)], aloc.at[p])

    def mate_a(p):
        return remote(
            act.at[:, pl.ds(pl.multiple_of((1 - c) * BLK + p * PW, PW), PW)], abuf.at[0, mine, cols(p)],
            ad2d_s.at[p], ad2d_r.at[p], mate)

    for p in range(NP):
        mate_a(p).start()
        local_a(p).start()
    g_local = pltpu.make_async_copy(og, gbuf.at[mine, own_cols], gloc)
    g_beside = remote(og, gbuf.at[mine, own_cols], gs.at[0], gr.at[0], beside)
    g_mate = remote(og, gbuf.at[mine, own_cols], gs.at[1], gr.at[1], mate)
    g_pass = remote(gbuf.at[mine, other_cols], gbuf.at[mine, other_cols], gs.at[2], gr.at[2], mate)
    g_local.start()
    g_beside.start()
    g_mate.start()

    def send_up(p):
        return remote(abuf.at[0, :, cols(p)], abuf.at[3, :, cols(p)], ys.at[0, p], yr.at[0, p], up)

    def send_down(p):
        return remote(abuf.at[0, :, cols(p)], abuf.at[1, :, cols(p)], ys.at[1, p], yr.at[1, p], down)

    def pass_down(p):
        return remote(
            abuf.at[1, 0:TOK, cols(p)], abuf.at[2, 0:TOK, cols(p)], ws.at[0, p], wr.at[0, p], down)

    def pass_up(p):
        return remote(
            abuf.at[3, TOK : 2 * TOK, cols(p)], abuf.at[2, TOK : 2 * TOK, cols(p)], ws.at[1, p], wr.at[1, p], up)

    def ready(p):
        local_a(p).wait()
        mate_a(p).wait_recv()

    for p in range(NP):
        ready(p)
        if p < 1:
            send_up(p).start()
            send_down(p).start()

    def factor_rows(p, carry):
        fs[cols(p), :] = contract0(abuf[0, :, cols(p)], abuf[0])
        return carry

    lax.fori_loop(0, NP, factor_rows, 0)
    fbuf[:, 48:64, :] = jnp.zeros((16, 16, BLK), bf16)

    def strips(r, carry):
        fbuf[r, 0:56, :] = fs[pl.ds(pl.multiple_of(r * 56, 8), 56), :].astype(bf16)
        return carry

    lax.fori_loop(0, 16, strips, 0)
    basis = pltpu.make_async_copy(basis_in.at[0], fs, qloc)
    basis.start()
    r1[...] = jnp.zeros_like(r1)
    g_local.wait()
    g_here = gbuf[mine, own_cols]
    obuf[...] = contract0(g_here, g_here).astype(bf16)

    theirs, ours = (1 - xh) * 8, xh * 8
    swap = (
        remote(fbuf.at[pl.ds(theirs, 8)], fswap, fss.at[0], frs.at[0], across),
        remote(obuf.at[pl.ds(pl.multiple_of(theirs * 32, 256), 256), :], oswap, oss.at[0], ors.at[0], across),
    )
    def strip(dz, cc):
        return ((z + dz) % 4) * 2 + (c + cc) % 2

    def send_strip(k):
        dz, cc = column[k - 1]
        to = device(xh, xl, y, z + dz, (c + cc) % 2)
        r = strip(dz, cc)
        return (
            remote(fswap.at[r], frecv.at[k], fss.at[k], frs.at[k], to),
            remote(oswap.at[pl.ds(pl.multiple_of(r * 32, 32), 32), :], orecv.at[k], oss.at[k], ors.at[k], to),
        )

    def send_strips():
        for copy in swap:
            copy.wait_recv()

        def add(r, carry):
            fswap[r] = (fswap[r].astype(f32) + fbuf[ours + r].astype(f32)).astype(bf16)
            return carry

        lax.fori_loop(0, 8, add, 0)
        oswap[...] = (oswap[...].astype(f32)
                      + obuf[pl.ds(pl.multiple_of(ours * 32, 256), 256), :].astype(f32)).astype(bf16)
        for k in range(1, 8):
            for copy in send_strip(k):
                copy.start()

    def partial(d, p, tx):
        e = (y - z + d + 4) % 4
        other = gbuf[:, pl.ds(pl.multiple_of(tx * ROWS, ROWS), ROWS)]
        pbuf[e, tx, cols(p), :] = contract0(abuf[d, :, cols(p)], other).astype(bf16)

    def hop1(p, tx):
        near = pl.ds(pl.multiple_of(p * PW, 64), 64)
        far = pl.ds(pl.multiple_of(p * PW + 64, 64), 64)
        rows = pl.ds(pl.multiple_of(p * 64, 64), 64)
        return (
            remote(pbuf.at[2, tx, near, :], h1.at[0, tx, rows, :], h1s.at[0, p, tx], h1r.at[0, p, tx], fore),
            remote(pbuf.at[2, tx, far, :], h1.at[1, tx, rows, :], h1s.at[1, p, tx], h1r.at[1, p, tx], back),
        )

    def hop2(p, tx):
        return (
            remote(pbuf.at[1, tx, cols(p), :], h2.at[0, tx, cols(p), :], h2s.at[0, p, tx], h2r.at[0, p, tx], fore),
            remote(pbuf.at[3, tx, cols(p), :], h2.at[1, tx, cols(p), :], h2s.at[1, p, tx], h2r.at[1, p, tx], back),
        )

    def add_hop1(p, tx):
        near = pl.ds(pl.multiple_of(p * PW, 64), 64)
        far = pl.ds(pl.multiple_of(p * PW + 64, 64), 64)
        rows = pl.ds(pl.multiple_of(p * 64, 64), 64)
        pbuf[1, tx, near, :] = (pbuf[1, tx, near, :].astype(f32) + h1[0, tx, rows, :].astype(f32)).astype(bf16)
        pbuf[3, tx, far, :] = (pbuf[3, tx, far, :].astype(f32) + h1[1, tx, rows, :].astype(f32)).astype(bf16)

    def to_owner(tx, p):
        return remote(
            sbuf.at[tx, cols(p), :], xr.at[xh, cols(p), :], xs.at[tx, p], xrs.at[xh, p], device(xl, tx, y, z, c))

    def from_half(kx, p):
        return remote(
            sbuf.at[0, cols(p), :], xr.at[kx, cols(p), :], xs.at[0, p], xrs.at[kx, p], beside)

    def is_self(tx):
        return jnp.logical_and(xh == xl, xl == tx)

    def comes_from_self(kx):
        return jnp.logical_and(xh == xl, kx == xh)

    own, oth = xl, 1 - xl

    def near_tail(p, tx):
        pass_down(p).wait_recv()
        pass_up(p).wait_recv()
        partial(2, p, tx)
        for copy in hop1(p, tx):
            copy.start()

    def step(i, carry):
        @pl.when(jnp.logical_and(i >= LAG2, i < NP + LAG2))
        def _():
            p = i - LAG2
            for tx in (own, oth):
                for copy in hop1(p, tx):
                    copy.wait_recv()
                add_hop1(p, tx)
                for copy in hop2(p, tx):
                    copy.start()

        @pl.when(i == 2)
        def _():
            basis.wait()

            def halves(p, carry):
                high, low = split(fs[cols(p), :])
                qh[cols(p), :] = high
                ql[cols(p), :] = low
                return carry

            lax.fori_loop(0, NP, halves, 0)

        @pl.when(i == STRIPS)
        def _():
            send_strips()

        @pl.when(i < NP)
        def _():
            @pl.when(i + 1 < NP)
            def _():
                send_up(i).wait_send()
                send_down(i).wait_send()
                send_up(i + 1).start()
                send_down(i + 1).start()

            send_down(i).wait_recv()
            pass_down(i).start()
            send_up(i).wait_recv()
            pass_up(i).start()

            @pl.when(i == 0)
            def _():
                g_mate.wait_recv()

            for d in (0, 1, 3):
                partial(d, i, own)

            @pl.when(i == 1)
            def _():
                g_pass.wait_recv()
                for d in (0, 1, 3):
                    partial(d, 0, oth)

            @pl.when(i >= 1)
            def _():
                for d in (0, 1, 3):
                    partial(d, i, oth)

            @pl.when(i == 0)
            def _():
                near_tail(0, own)
                g_beside.wait_recv()
                g_pass.start()
                for copy in swap:
                    copy.start()

        @pl.when(jnp.logical_and(i >= 1, i < NP + 1))
        def _():
            p = i - 1

            @pl.when(i > 1)
            def _():
                near_tail(p, own)

            partial(2, p, oth)
            for copy in hop1(p, oth):
                copy.start()

        @pl.when(jnp.logical_and(i >= LAG3, i < NP + LAG3))
        def _():
            p = i - LAG3
            for tx in range(2):
                for copy in hop2(p, tx):
                    copy.wait_recv()
                total = (pbuf[0, tx, cols(p), :].astype(f32) + h2[0, tx, cols(p), :].astype(f32)
                         + h2[1, tx, cols(p), :].astype(f32))
                sbuf[tx, cols(p), :] = total.astype(bf16)

                @pl.when(is_self(tx))
                def _():
                    xr[xh, cols(p), :] = total.astype(bf16)

                @pl.when(jnp.logical_not(is_self(tx)))
                def _():
                    to_owner(tx, p).start()

        @pl.when(i >= LAG4)
        def _():
            p = i - LAG4
            for kx in range(2):
                @pl.when(jnp.logical_not(comes_from_self(kx)))
                def _():
                    from_half(kx, p).wait_recv()
            high, low = split((xr[0, cols(p), :].astype(f32) + xr[1, cols(p), :].astype(f32)) * SCALE)
            left = jnp.concatenate([qh[cols(p), :], ql[cols(p), :], qh[cols(p), :]], axis=0)
            right = jnp.concatenate([high, high, low], axis=0)
            r1[...] += contract0(left, right)

        return carry

    lax.fori_loop(0, NP + LAG4, step, 0)

    oh, ol = split(basis_out[...])
    for start, size in (FIRST, LAST):
        rows = slice(start, start + size)
        mh, ml = split(r1[rows, :])
        turned = dot(mh, oh) + dot(mh, ol) + dot(ml, oh)
        for p in range(start // 128, (start + size) // 128):
            spread = jnp.transpose(jnp.broadcast_to(eigen_in[p : p + 1, :], (128, 128)))
            for k in range(ROWS // 128):
                lanes = slice(k * 128, (k + 1) * 128)
                scaled = turned[p * 128 - start : (p + 1) * 128 - start, lanes] / (
                    spread * eigen_out[:, lanes] + damping)
                vbuf[p * 128 : (p + 1) * 128, lanes] = scaled.astype(bf16)
        back_out = lax.dot_general(
            vbuf[rows, :], oh, (((1,), (1,)), ((), ())), preferred_element_type=f32)
        vbuf[rows, :] = back_out.astype(bf16)

    def part(other, dz, core, start, size):
        half = (1 - xh) if other else xh
        base = (half * 8 + ((z + dz) % 4) * 2 + core) * BLK
        return u.at[pl.ds(pl.multiple_of(base + start, 64), size), :]

    def hand(other, dz, start, size, ssem, rsem, to):
        return remote(part(other, dz, c, start, size), part(other, dz, c, start, size), ssem, rsem, to)

    waits = []

    def go(descriptor):
        descriptor.start()
        waits.append(descriptor)
        return descriptor

    def ring(sem, other, start, size):
        go(hand(other, 0, start, size, zs.at[0, sem], zr.at[0, sem], fore))
        go(hand(other, 0, start, size, zs.at[1, sem], zr.at[1, sem], back))

    def ring_take(sem, other, start, size):
        hand(other, 3, start, size, zs.at[0, sem], zr.at[0, sem], fore).wait_recv()
        hand(other, 1, start, size, zs.at[1, sem], zr.at[1, sem], back).wait_recv()

    def relay(sem, other, start, size):
        half = size // 2
        go(hand(other, 3, start, half, vs.at[0, sem], vr.at[0, sem], fore))
        go(hand(other, 1, start + half, half, vs.at[1, sem], vr.at[1, sem], back))

    def relay_take(sem, other, start, size):
        half = size // 2
        hand(other, 2, start, half, vs.at[0, sem], vr.at[0, sem], fore).wait_recv()
        hand(other, 2, start + half, half, vs.at[1, sem], vr.at[1, sem], back).wait_recv()

    def cross(sem, dz, start, size):
        go(hand(False, dz, start, size, cs.at[sem], cr.at[sem], across))

    def cross_take(sem, dz, start, size):
        hand(True, dz, start, size, cs.at[sem], cr.at[sem], across).wait_recv()

    given = []

    def share(other, dz, start, size):
        sem = len(given)
        go(hand(other, dz, start, size, ds.at[sem], dr.at[sem], mate))
        given.append((other, dz, start, size))

    for k, (start, size) in enumerate(PARTS):
        block = dot(qh[start : start + size, :], vbuf[...]).astype(bf16)
        u[pl.ds(pl.multiple_of(me * BLK + start, 64), size), :] = block
        if k < 2:
            cross(k, 0, start, size)
            ring(k, False, start, size)
        if k == 3:
            ring(2, False, *LAST)
            cross(2, 0, *LAST)
    share(False, 0, *FIRST)
    share(False, 0, *LAST)
    for k in range(1, 8):
        for copy in send_strip(k):
            copy.wait_recv()
    here = fswap[z * 2 + c, 0:56, :].astype(f32)
    for k in range(1, 4):
        here += frecv[k, 0:56, :].astype(f32)
    there = frecv[4, 0:56, :].astype(f32)
    for k in range(5, 8):
        there += frecv[k, 0:56, :].astype(f32)
    fin_out[c] = here * SCALE
    fin_out[1 - c] = there * SCALE
    total = oswap[pl.ds(pl.multiple_of((z * 2 + c) * 32, 32), 32), :].astype(f32)
    for k in range(1, 8):
        total += orecv[k].astype(f32)
    fout_out[...] = total * SCALE

    for k in range(2):
        ring_take(k, False, *PARTS[k])
        relay(k, False, *PARTS[k])
    for k in range(2):
        cross_take(k, 0, *PARTS[k])
        ring(3 + k, True, *PARTS[k])
    ring_take(2, False, *LAST)
    relay(2, False, *LAST)
    cross(3, 1, *LAST)
    cross(4, 3, *LAST)
    for dz in (1, 3):
        share(False, dz, 0, BLK)
    share(True, 0, *FIRST)
    for k in range(2):
        relay_take(k, False, *PARTS[k])
    share(False, 2, *FIRST)
    relay_take(2, False, *LAST)
    cross(5, 2, *LAST)
    share(False, 2, *LAST)
    cross_take(2, 0, *LAST)
    share(True, 0, *LAST)
    for k in range(2):
        ring_take(3 + k, True, *PARTS[k])
        relay(3 + k, True, *PARTS[k])
    share(True, 1, *FIRST)
    share(True, 3, *FIRST)
    cross_take(3, 1, *LAST)
    share(True, 1, *LAST)
    cross_take(4, 3, *LAST)
    share(True, 3, *LAST)
    cross_take(5, 2, *LAST)
    share(True, 2, *LAST)
    for k in range(2):
        relay_take(3 + k, True, *PARTS[k])
        share(True, 2, *PARTS[k])
    for sem, (other, dz, start, size) in enumerate(given):
        ref = part(other, dz, 1 - c, start, size)
        remote(ref, ref, ds.at[sem], dr.at[sem], mate).wait_recv()
    for descriptor in waits:
        descriptor.wait_send()

    for copy in (g_beside, g_mate, g_pass):
        copy.wait_send()

    def finish(p, carry):
        mate_a(p).wait_send()
        for copy in (pass_down(p), pass_up(p)):
            copy.wait_send()
        for tx in range(2):
            for copy in hop1(p, tx) + hop2(p, tx):
                copy.wait_send()

            @pl.when(jnp.logical_not(is_self(tx)))
            def _():
                to_owner(tx, p).wait_send()
        return carry

    lax.fori_loop(0, NP, finish, 0)
    for p in range(NP - 1, NP):
        send_up(p).wait_send()
        send_down(p).wait_send()

    for copy in swap:
        copy.wait_send()
    for k in range(1, 8):
        for copy in send_strip(k):
            copy.wait_send()


def whole_step(activations, output_grads, basis_in, eigen_in, basis_out, eigen_out):
    dma = pltpu.SemaphoreType.DMA
    any_spec = pl.BlockSpec(memory_space=pl.ANY)
    vmem = pl.BlockSpec(memory_space=pltpu.VMEM)
    return pl.pallas_call(
        step_kernel,
        out_shape=(
            pltpu.VMEM((16 * BLK, ROWS), bf16),
            jax.ShapeDtypeStruct((2, 56, BLK), f32),
            jax.ShapeDtypeStruct((32, ROWS), f32),
        ),
        in_specs=[any_spec, any_spec, any_spec, vmem, vmem, vmem],
        out_specs=(vmem, vmem, vmem),
        scratch_shapes=[
            pltpu.VMEM((4, 2 * TOK, BLK), bf16),
            pltpu.VMEM((2 * TOK, 2 * ROWS), bf16),
            pltpu.VMEM((4, 2, BLK, ROWS), bf16),
            pltpu.VMEM((2, 2, BLK // 2, ROWS), bf16),
            pltpu.VMEM((2, 2, BLK, ROWS), bf16),
            pltpu.VMEM((2, BLK, ROWS), bf16),
            pltpu.VMEM((2, BLK, ROWS), bf16),
            pltpu.VMEM((BLK, BLK), f32),
            pltpu.VMEM((16, 64, BLK), bf16),
            pltpu.VMEM((8, 64, BLK), bf16),
            pltpu.VMEM((8, 64, BLK), bf16),
            pltpu.VMEM((ROWS, ROWS), bf16),
            pltpu.VMEM((ROWS // 2, ROWS), bf16),
            pltpu.VMEM((8, 32, ROWS), bf16),
            dma((NP,)), dma((NP,)), dma((NP,)),
            dma, dma((3,)), dma((3,)),
            dma((2, NP)), dma((2, NP)), dma((2, NP)), dma((2, NP)),
            dma((2, NP, 2)), dma((2, NP, 2)), dma((2, NP, 2)), dma((2, NP, 2)),
            dma((2, NP)), dma((2, NP)),
            dma((8,)), dma((8,)), dma((8,)), dma((8,)),
            pltpu.VMEM((BLK, BLK), bf16),
            pltpu.VMEM((BLK, BLK), bf16),
            pltpu.VMEM((BLK, ROWS), f32),
            pltpu.VMEM((BLK, ROWS), bf16),
            dma,
            dma((2, 5)), dma((2, 5)), dma((2, 5)), dma((2, 5)),
            dma((6,)), dma((6,)), dma((20,)), dma((20,)),
        ],
        compiler_params=pltpu.CompilerParams(
            collective_id=0, has_side_effects=True, vmem_limit_bytes=48 * 2**20),
        cost_estimate=pl.CostEstimate(flops=15_000_000_000, bytes_accessed=26_000_000, transcendentals=0),
        name="kfac_step",
    )(activations, output_grads, basis_in, eigen_in, basis_out, eigen_out)


def body(activations, output_grads, basis_in, eigen_in, basis_out, eigen_out):
    update, fin, factor_out = whole_step(
        activations, output_grads, basis_in, eigen_in.reshape(NP, PW), basis_out, eigen_out.reshape(1, ROWS))
    return (update, jnp.transpose(fin, (1, 0, 2)), factor_out)


def solution(mesh):
    in_specs = (
        P("dp", "tensor"),
        P("dp", "tensor"),
        P("dp", None, None),
        P("dp"),
        P("tensor", None),
        P("tensor"),
    )
    out_specs = (P(None, "tensor"), P("dp", "tensor", None), P("dp", "tensor"))
    return jax.shard_map(body, mesh=mesh, in_specs=in_specs, out_specs=out_specs, check_vma=False)
```

```python
import functools
import jax
import jax.numpy as jnp
from jax import lax
from jax.experimental import pallas as pl
from jax.experimental.pallas import tpu as pltpu
from jax.sharding import PartitionSpec as P

MESH = pl.DeviceIdType.MESH
BLK = 896
ROWS = 512
TOK = 512
NP = 7
PW = 128
SCALE = 1.0 / 8192
LAG2, LAG3, LAG4 = 2, 3, 6
STRIPS = NP - 1 + LAG2
AHEAD, RELAYS = 1, 1
damping = 0.01
f32, bf16 = jnp.float32, jnp.bfloat16


def where():
    dp, t = lax.axis_index("dp"), lax.axis_index("tensor")
    return dp // 8, t // 4, t % 4, (dp // 2) % 4, dp % 2


def device(xh, xl, y, z, c):
    return (xh * 8 + (z % 4) * 2 + c, xl * 4 + (y % 4))


def contract0(a, b):
    return lax.dot_general(a, b, (((0,), (0,)), ((), ())), preferred_element_type=f32)


def remote(src, dst, ssem, rsem, to):
    return pltpu.make_async_remote_copy(
        src_ref=src, dst_ref=dst, send_sem=ssem, recv_sem=rsem, device_id=to, device_id_type=MESH
    )


def greet(peers):
    barrier = pltpu.get_barrier_semaphore()
    for peer in peers:
        pl.semaphore_signal(barrier, inc=1, device_id=peer, device_id_type=MESH)
    pl.semaphore_wait(barrier, len(peers))


def split(x):
    high = x.astype(bf16)
    return high, (x - high.astype(f32)).astype(bf16)


def dot(a, b):
    return jnp.dot(a, b, preferred_element_type=f32)


PARTS = ((0, 256), (256, 256), (512, 192), (704, 192))
FIRST = (0, 512)
LAST = (512, 384)


def step_kernel(
    act, og, basis_in, eigen_in, basis_out, eigen_out, u, fin_out, fout_out,
    abuf, gbuf, pbuf, h1, h2, sbuf, xr, fs, fbuf, fswap, frecv, obuf, oswap, orecv,
    aloc, ad2d_s, ad2d_r, gloc, gs, gr, ys, yr, ws, wr, h1s, h1r, h2s, h2r, xs, xrs, fss, frs, oss, ors,
    qh, ql, r1, vbuf, qloc, zs, zr, vs, vr, cs, cr, ds, dr,
):
    xh, xl, y, z, c = where()
    me = xh * 8 + z * 2 + c
    mate = device(xh, xl, y, z, 1 - c)
    up, down = device(xh, xl, y + 1, z, c), device(xh, xl, y + 3, z, c)
    fore, back = device(xh, xl, y, z + 1, c), device(xh, xl, y, z + 3, c)
    beside = device(xh, 1 - xl, y, z, c)
    across = device(1 - xh, xl, y, z, c)
    column = [(dz, cc) for cc in range(2) for dz in range(4)][1:]
    peers = [device(xh, xl, y, z + dz, (c + cc) % 2) for dz, cc in column]
    greet(peers + [up, down, beside, across, device(1 - xh, 1 - xl, y, z, c)])

    mine = pl.ds(pl.multiple_of(c * TOK, TOK), TOK)
    own_cols = pl.ds(pl.multiple_of(xl * ROWS, ROWS), ROWS)
    other_cols = pl.ds(pl.multiple_of((1 - xl) * ROWS, ROWS), ROWS)

    def cols(p):
        return pl.ds(pl.multiple_of(p * PW, PW), PW)

    def local_a(p):
        return pltpu.make_async_copy(
            act.at[:, pl.ds(pl.multiple_of(c * BLK + p * PW, PW), PW)], abuf.at[0, mine, cols(p)], aloc.at[p])

    def mate_a(p):
        return remote(
            act.at[:, pl.ds(pl.multiple_of((1 - c) * BLK + p * PW, PW), PW)], abuf.at[0, mine, cols(p)],
            ad2d_s.at[p], ad2d_r.at[p], mate)

    for p in range(NP):
        mate_a(p).start()
        local_a(p).start()
    g_local = pltpu.make_async_copy(og, gbuf.at[mine, own_cols], gloc)
    g_beside = remote(og, gbuf.at[mine, own_cols], gs.at[0], gr.at[0], beside)
    g_mate = remote(og, gbuf.at[mine, own_cols], gs.at[1], gr.at[1], mate)
    g_pass = remote(gbuf.at[mine, other_cols], gbuf.at[mine, other_cols], gs.at[2], gr.at[2], mate)
    g_local.start()
    g_beside.start()
    g_mate.start()

    theirs_too = pl.ds(pl.multiple_of((1 - c) * TOK, TOK), TOK)

    def rounds(p):
        out = []
        for k, rows in enumerate((mine, theirs_too)):
            out.append(remote(
                abuf.at[0, rows, cols(p)], abuf.at[3, rows, cols(p)], ys.at[0, p, k], yr.at[0, p, k], up))
            out.append(remote(
                abuf.at[0, rows, cols(p)], abuf.at[1, rows, cols(p)], ys.at[1, p, k], yr.at[1, p, k], down))
        return tuple(out)

    def relays(p, first, second):
        out = []
        for k in range(RELAYS):
            size = TOK // RELAYS
            low, high = pl.ds(k * size, size), pl.ds(TOK + k * size, size)
            if first:
                out.append(remote(
                    abuf.at[1, low, cols(p)], abuf.at[2, low, cols(p)], ws.at[0, p, k], wr.at[0, p, k], down))
            if second:
                out.append(remote(
                    abuf.at[3, high, cols(p)], abuf.at[2, high, cols(p)], ws.at[1, p, k], wr.at[1, p, k], up))
        return tuple(out)

    for p in range(NP):
        local_a(p).wait()
        if p == 0:
            for copy in rounds(p)[:2]:
                copy.start()
        mate_a(p).wait_recv()
        if p < AHEAD:
            for copy in rounds(p)[2 * (p == 0):]:
                copy.start()

    def factor_rows(p, carry):
        fs[cols(p), :] = contract0(abuf[0, :, cols(p)], abuf[0])
        return carry

    lax.fori_loop(0, NP, factor_rows, 0)
    fbuf[:, 48:64, :] = jnp.zeros((16, 16, BLK), bf16)

    def strips(r, carry):
        fbuf[r, 0:56, :] = fs[pl.ds(pl.multiple_of(r * 56, 8), 56), :].astype(bf16)
        return carry

    lax.fori_loop(0, 16, strips, 0)
    basis = pltpu.make_async_copy(basis_in.at[0], fs, qloc)
    basis.start()
    r1[...] = jnp.zeros_like(r1)
    g_local.wait()
    g_here = gbuf[mine, own_cols]
    obuf[...] = contract0(g_here, g_here).astype(bf16)

    theirs, ours = (1 - xh) * 8, xh * 8
    swap = (
        remote(fbuf.at[pl.ds(theirs, 8)], fswap, fss.at[0], frs.at[0], across),
        remote(obuf.at[pl.ds(pl.multiple_of(theirs * 32, 256), 256), :], oswap, oss.at[0], ors.at[0], across),
    )
    def strip(dz, cc):
        return ((z + dz) % 4) * 2 + (c + cc) % 2

    def send_strip(k):
        dz, cc = column[k - 1]
        to = device(xh, xl, y, z + dz, (c + cc) % 2)
        r = strip(dz, cc)
        return (
            remote(fswap.at[r], frecv.at[k], fss.at[k], frs.at[k], to),
            remote(oswap.at[pl.ds(pl.multiple_of(r * 32, 32), 32), :], orecv.at[k], oss.at[k], ors.at[k], to),
        )

    def send_strips():
        for copy in swap:
            copy.wait_recv()

        def add(r, carry):
            fswap[r] = (fswap[r].astype(f32) + fbuf[ours + r].astype(f32)).astype(bf16)
            return carry

        lax.fori_loop(0, 8, add, 0)
        oswap[...] = (oswap[...].astype(f32)
                      + obuf[pl.ds(pl.multiple_of(ours * 32, 256), 256), :].astype(f32)).astype(bf16)
        for k in range(1, 8):
            for copy in send_strip(k):
                copy.start()

    def partial(d, p, tx):
        e = (y - z + d + 4) % 4
        other = gbuf[:, pl.ds(pl.multiple_of(tx * ROWS, ROWS), ROWS)]
        pbuf[e, tx, cols(p), :] = contract0(abuf[d, :, cols(p)], other).astype(bf16)

    def hop1(p, tx):
        near = pl.ds(pl.multiple_of(p * PW, 64), 64)
        far = pl.ds(pl.multiple_of(p * PW + 64, 64), 64)
        rows = pl.ds(pl.multiple_of(p * 64, 64), 64)
        return (
            remote(pbuf.at[2, tx, near, :], h1.at[0, tx, rows, :], h1s.at[0, p, tx], h1r.at[0, p, tx], fore),
            remote(pbuf.at[2, tx, far, :], h1.at[1, tx, rows, :], h1s.at[1, p, tx], h1r.at[1, p, tx], back),
        )

    def hop2(p, tx):
        return (
            remote(pbuf.at[1, tx, cols(p), :], h2.at[0, tx, cols(p), :], h2s.at[0, p, tx], h2r.at[0, p, tx], fore),
            remote(pbuf.at[3, tx, cols(p), :], h2.at[1, tx, cols(p), :], h2s.at[1, p, tx], h2r.at[1, p, tx], back),
        )

    def add_hop1(p, tx):
        near = pl.ds(pl.multiple_of(p * PW, 64), 64)
        far = pl.ds(pl.multiple_of(p * PW + 64, 64), 64)
        rows = pl.ds(pl.multiple_of(p * 64, 64), 64)
        pbuf[1, tx, near, :] = (pbuf[1, tx, near, :].astype(f32) + h1[0, tx, rows, :].astype(f32)).astype(bf16)
        pbuf[3, tx, far, :] = (pbuf[3, tx, far, :].astype(f32) + h1[1, tx, rows, :].astype(f32)).astype(bf16)

    def to_owner(tx, p):
        return remote(
            sbuf.at[tx, cols(p), :], xr.at[xh, cols(p), :], xs.at[tx, p], xrs.at[xh, p], device(xl, tx, y, z, c))

    def from_half(kx, p):
        return remote(
            sbuf.at[0, cols(p), :], xr.at[kx, cols(p), :], xs.at[0, p], xrs.at[kx, p], beside)

    def is_self(tx):
        return jnp.logical_and(xh == xl, xl == tx)

    def comes_from_self(kx):
        return jnp.logical_and(xh == xl, kx == xh)

    own, oth = xl, 1 - xl

    def product(d, p, tx):
        partial(d, p, tx)

        @pl.when((y - z + d + 4) % 4 == 2)
        def _():
            for copy in hop1(p, tx):
                copy.start()

    def near_tail(p, tx):
        for copy in relays(p, True, True):
            copy.wait_recv()
        product(2, p, tx)

    def step(i, carry):
        @pl.when(jnp.logical_and(i >= LAG2, i < NP + LAG2))
        def _():
            p = i - LAG2
            for tx in (own, oth):
                for copy in hop1(p, tx):
                    copy.wait_recv()
                add_hop1(p, tx)
                for copy in hop2(p, tx):
                    copy.start()

        @pl.when(i < NP)
        def _():
            @pl.when(i + AHEAD < NP)
            def _():
                for copy in rounds(i):
                    copy.wait_send()
                for copy in rounds(i + AHEAD):
                    copy.start()

            arrivals = rounds(i)
            for k in (1, 3):
                arrivals[k].wait_recv()
            for copy in relays(i, True, False):
                copy.start()
            for k in (0, 2):
                arrivals[k].wait_recv()
            for copy in relays(i, False, True):
                copy.start()

            @pl.when(i == 0)
            def _():
                g_mate.wait_recv()

            for d in (0, 1, 3):
                product(d, i, own)

            @pl.when(i == 1)
            def _():
                g_pass.wait_recv()
                for d in (0, 1, 3):
                    product(d, 0, oth)

            @pl.when(i >= 1)
            def _():
                for d in (0, 1, 3):
                    product(d, i, oth)

            @pl.when(i == 0)
            def _():
                g_beside.wait_recv()
                g_pass.start()
                for copy in swap:
                    copy.start()
                near_tail(0, own)

        @pl.when(jnp.logical_and(i >= 1, i < NP + 1))
        def _():
            p = i - 1

            @pl.when(i > 1)
            def _():
                near_tail(p, own)

            product(2, p, oth)

        @pl.when(jnp.logical_and(i >= LAG3, i < NP + LAG3))
        def _():
            p = i - LAG3
            for tx in range(2):
                for copy in hop2(p, tx):
                    copy.wait_recv()
                total = (pbuf[0, tx, cols(p), :].astype(f32) + h2[0, tx, cols(p), :].astype(f32)
                         + h2[1, tx, cols(p), :].astype(f32))
                sbuf[tx, cols(p), :] = total.astype(bf16)

                @pl.when(is_self(tx))
                def _():
                    xr[xh, cols(p), :] = total.astype(bf16)

                @pl.when(jnp.logical_not(is_self(tx)))
                def _():
                    to_owner(tx, p).start()

        @pl.when(i == 2)
        def _():
            basis.wait()

            def halves(p, carry):
                high, low = split(fs[cols(p), :])
                qh[cols(p), :] = high
                ql[cols(p), :] = low
                return carry

            lax.fori_loop(0, NP, halves, 0)

        @pl.when(i == STRIPS)
        def _():
            send_strips()

        @pl.when(i >= LAG4)
        def _():
            p = i - LAG4
            for kx in range(2):
                @pl.when(jnp.logical_not(comes_from_self(kx)))
                def _():
                    from_half(kx, p).wait_recv()
            high, low = split((xr[0, cols(p), :].astype(f32) + xr[1, cols(p), :].astype(f32)) * SCALE)
            left = jnp.concatenate([qh[cols(p), :], ql[cols(p), :], qh[cols(p), :]], axis=0)
            right = jnp.concatenate([high, high, low], axis=0)
            r1[...] += contract0(left, right)

        return carry

    lax.fori_loop(0, NP + LAG4, step, 0)

    oh, ol = split(basis_out[...])
    for start, size in (FIRST, LAST):
        rows = slice(start, start + size)
        mh, ml = split(r1[rows, :])
        turned = dot(mh, oh) + dot(mh, ol) + dot(ml, oh)
        for p in range(start // 128, (start + size) // 128):
            spread = jnp.transpose(jnp.broadcast_to(eigen_in[p : p + 1, :], (128, 128)))
            for k in range(ROWS // 128):
                lanes = slice(k * 128, (k + 1) * 128)
                scaled = turned[p * 128 - start : (p + 1) * 128 - start, lanes] / (
                    spread * eigen_out[:, lanes] + damping)
                vbuf[p * 128 : (p + 1) * 128, lanes] = scaled.astype(bf16)
        back_out = lax.dot_general(
            vbuf[rows, :], oh, (((1,), (1,)), ((), ())), preferred_element_type=f32)
        vbuf[rows, :] = back_out.astype(bf16)

    def part(other, dz, core, start, size):
        half = (1 - xh) if other else xh
        base = (half * 8 + ((z + dz) % 4) * 2 + core) * BLK
        return u.at[pl.ds(pl.multiple_of(base + start, 64), size), :]

    def hand(other, dz, start, size, ssem, rsem, to):
        return remote(part(other, dz, c, start, size), part(other, dz, c, start, size), ssem, rsem, to)

    waits = []

    def go(descriptor):
        descriptor.start()
        waits.append(descriptor)
        return descriptor

    def ring(sem, other, start, size):
        go(hand(other, 0, start, size, zs.at[0, sem], zr.at[0, sem], fore))
        go(hand(other, 0, start, size, zs.at[1, sem], zr.at[1, sem], back))

    def ring_take(sem, other, start, size):
        hand(other, 3, start, size, zs.at[0, sem], zr.at[0, sem], fore).wait_recv()
        hand(other, 1, start, size, zs.at[1, sem], zr.at[1, sem], back).wait_recv()

    def relay(sem, other, start, size):
        half = size // 2
        go(hand(other, 3, start, half, vs.at[0, sem], vr.at[0, sem], fore))
        go(hand(other, 1, start + half, half, vs.at[1, sem], vr.at[1, sem], back))

    def relay_take(sem, other, start, size):
        half = size // 2
        hand(other, 2, start, half, vs.at[0, sem], vr.at[0, sem], fore).wait_recv()
        hand(other, 2, start + half, half, vs.at[1, sem], vr.at[1, sem], back).wait_recv()

    def cross(sem, dz, start, size):
        go(hand(False, dz, start, size, cs.at[sem], cr.at[sem], across))

    def cross_take(sem, dz, start, size):
        hand(True, dz, start, size, cs.at[sem], cr.at[sem], across).wait_recv()

    given = []

    def share(other, dz, start, size):
        sem = len(given)
        go(hand(other, dz, start, size, ds.at[sem], dr.at[sem], mate))
        given.append((other, dz, start, size))

    for k, (start, size) in enumerate(PARTS):
        block = dot(qh[start : start + size, :], vbuf[...]).astype(bf16)
        u[pl.ds(pl.multiple_of(me * BLK + start, 64), size), :] = block
        if k < 2:
            cross(k, 0, start, size)
            ring(k, False, start, size)
        if k == 3:
            ring(2, False, *LAST)
            cross(2, 0, *LAST)
    share(False, 0, *FIRST)
    share(False, 0, *LAST)
    for k in range(2):
        ring_take(k, False, *PARTS[k])
        relay(k, False, *PARTS[k])
    for k in range(2):
        cross_take(k, 0, *PARTS[k])
        ring(3 + k, True, *PARTS[k])
    ring_take(2, False, *LAST)
    relay(2, False, *LAST)
    cross(3, 1, *LAST)
    cross(4, 3, *LAST)
    for dz in (1, 3):
        share(False, dz, 0, BLK)
    share(True, 0, *FIRST)
    for k in range(2):
        relay_take(k, False, *PARTS[k])
    share(False, 2, *FIRST)
    relay_take(2, False, *LAST)
    cross(5, 2, *LAST)
    share(False, 2, *LAST)
    cross_take(2, 0, *LAST)
    share(True, 0, *LAST)
    for k in range(2):
        ring_take(3 + k, True, *PARTS[k])
        relay(3 + k, True, *PARTS[k])
    share(True, 1, *FIRST)
    share(True, 3, *FIRST)
    cross_take(3, 1, *LAST)
    share(True, 1, *LAST)
    cross_take(4, 3, *LAST)
    share(True, 3, *LAST)
    cross_take(5, 2, *LAST)
    share(True, 2, *LAST)
    for k in range(2):
        relay_take(3 + k, True, *PARTS[k])
        share(True, 2, *PARTS[k])
    for k in range(1, 8):
        for copy in send_strip(k):
            copy.wait_recv()
    here = fswap[z * 2 + c, 0:56, :].astype(f32)
    for k in range(1, 4):
        here += frecv[k, 0:56, :].astype(f32)
    there = frecv[4, 0:56, :].astype(f32)
    for k in range(5, 8):
        there += frecv[k, 0:56, :].astype(f32)
    fin_out[c] = here * SCALE
    fin_out[1 - c] = there * SCALE
    total = oswap[pl.ds(pl.multiple_of((z * 2 + c) * 32, 32), 32), :].astype(f32)
    for k in range(1, 8):
        total += orecv[k].astype(f32)
    fout_out[...] = total * SCALE

    for sem, (other, dz, start, size) in enumerate(given):
        ref = part(other, dz, 1 - c, start, size)
        remote(ref, ref, ds.at[sem], dr.at[sem], mate).wait_recv()
    for descriptor in waits:
        descriptor.wait_send()

    for copy in (g_beside, g_mate, g_pass):
        copy.wait_send()

    def finish(p, carry):
        mate_a(p).wait_send()
        for copy in relays(p, True, True):
            copy.wait_send()
        for tx in range(2):
            for copy in hop1(p, tx) + hop2(p, tx):
                copy.wait_send()

            @pl.when(jnp.logical_not(is_self(tx)))
            def _():
                to_owner(tx, p).wait_send()
        return carry

    lax.fori_loop(0, NP, finish, 0)
    for p in range(NP - AHEAD, NP):
        for copy in rounds(p):
            copy.wait_send()

    for copy in swap:
        copy.wait_send()
    for k in range(1, 8):
        for copy in send_strip(k):
            copy.wait_send()


def whole_step(activations, output_grads, basis_in, eigen_in, basis_out, eigen_out):
    dma = pltpu.SemaphoreType.DMA
    any_spec = pl.BlockSpec(memory_space=pl.ANY)
    vmem = pl.BlockSpec(memory_space=pltpu.VMEM)
    return pl.pallas_call(
        step_kernel,
        out_shape=(
            pltpu.VMEM((16 * BLK, ROWS), bf16),
            jax.ShapeDtypeStruct((2, 56, BLK), f32),
            jax.ShapeDtypeStruct((32, ROWS), f32),
        ),
        in_specs=[any_spec, any_spec, any_spec, vmem, vmem, vmem],
        out_specs=(vmem, vmem, vmem),
        scratch_shapes=[
            pltpu.VMEM((4, 2 * TOK, BLK), bf16),
            pltpu.VMEM((2 * TOK, 2 * ROWS), bf16),
            pltpu.VMEM((4, 2, BLK, ROWS), bf16),
            pltpu.VMEM((2, 2, BLK // 2, ROWS), bf16),
            pltpu.VMEM((2, 2, BLK, ROWS), bf16),
            pltpu.VMEM((2, BLK, ROWS), bf16),
            pltpu.VMEM((2, BLK, ROWS), bf16),
            pltpu.VMEM((BLK, BLK), f32),
            pltpu.VMEM((16, 64, BLK), bf16),
            pltpu.VMEM((8, 64, BLK), bf16),
            pltpu.VMEM((8, 64, BLK), bf16),
            pltpu.VMEM((ROWS, ROWS), bf16),
            pltpu.VMEM((ROWS // 2, ROWS), bf16),
            pltpu.VMEM((8, 32, ROWS), bf16),
            dma((NP,)), dma((NP,)), dma((NP,)),
            dma, dma((3,)), dma((3,)),
            dma((2, NP, 2)), dma((2, NP, 2)), dma((2, NP, RELAYS)), dma((2, NP, RELAYS)),
            dma((2, NP, 2)), dma((2, NP, 2)), dma((2, NP, 2)), dma((2, NP, 2)),
            dma((2, NP)), dma((2, NP)),
            dma((8,)), dma((8,)), dma((8,)), dma((8,)),
            pltpu.VMEM((BLK, BLK), bf16),
            pltpu.VMEM((BLK, BLK), bf16),
            pltpu.VMEM((BLK, ROWS), f32),
            pltpu.VMEM((BLK, ROWS), bf16),
            dma,
            dma((2, 5)), dma((2, 5)), dma((2, 5)), dma((2, 5)),
            dma((6,)), dma((6,)), dma((20,)), dma((20,)),
        ],
        compiler_params=pltpu.CompilerParams(
            collective_id=0, has_side_effects=True, vmem_limit_bytes=48 * 2**20),
        cost_estimate=pl.CostEstimate(flops=15_000_000_000, bytes_accessed=26_000_000, transcendentals=0),
        name="kfac_step",
    )(activations, output_grads, basis_in, eigen_in, basis_out, eigen_out)


def body(activations, output_grads, basis_in, eigen_in, basis_out, eigen_out):
    update, fin, factor_out = whole_step(
        activations, output_grads, basis_in, eigen_in.reshape(NP, PW), basis_out, eigen_out.reshape(1, ROWS))
    return (update, jnp.transpose(fin, (1, 0, 2)), factor_out)


def solution(mesh):
    in_specs = (
        P("dp", "tensor"),
        P("dp", "tensor"),
        P("dp", None, None),
        P("dp"),
        P("tensor", None),
        P("tensor"),
    )
    out_specs = (P(None, "tensor"), P("dp", "tensor", None), P("dp", "tensor"))
    return jax.shard_map(body, mesh=mesh, in_specs=in_specs, out_specs=out_specs, check_vma=False)
```

```python
import functools
import jax
import jax.numpy as jnp
from jax import lax
from jax.experimental import pallas as pl
from jax.experimental.pallas import tpu as pltpu
from jax.sharding import PartitionSpec as P

MESH = pl.DeviceIdType.MESH
BLK = 896
ROWS = 512
TOK = 512
NP = 7
PW = 128
SCALE = 1.0 / 8192
LAG2, LAG3, LAG4 = 2, 3, 6
STRIPS = NP - 1 + LAG2
AHEAD, RELAYS = 1, 1
damping = 0.01
f32, bf16 = jnp.float32, jnp.bfloat16


def where():
    dp, t = lax.axis_index("dp"), lax.axis_index("tensor")
    return dp // 8, t // 4, t % 4, (dp // 2) % 4, dp % 2


def device(xh, xl, y, z, c):
    return (xh * 8 + (z % 4) * 2 + c, xl * 4 + (y % 4))


def contract0(a, b):
    return lax.dot_general(a, b, (((0,), (0,)), ((), ())), preferred_element_type=f32)


def remote(src, dst, ssem, rsem, to):
    return pltpu.make_async_remote_copy(
        src_ref=src, dst_ref=dst, send_sem=ssem, recv_sem=rsem, device_id=to, device_id_type=MESH
    )


def greet(peers):
    barrier = pltpu.get_barrier_semaphore()
    for peer in peers:
        pl.semaphore_signal(barrier, inc=1, device_id=peer, device_id_type=MESH)
    pl.semaphore_wait(barrier, len(peers))


def split(x):
    high = x.astype(bf16)
    return high, (x - high.astype(f32)).astype(bf16)


def dot(a, b):
    return jnp.dot(a, b, preferred_element_type=f32)


PARTS = ((0, 256), (256, 256), (512, 192), (704, 192))
FIRST = (0, 512)
LAST = (512, 384)


def step_kernel(
    act, og, basis_in, eigen_in, basis_out, eigen_out, u, fin_out, fout_out,
    abuf, gbuf, pbuf, h1, h2, sbuf, xr, fs, fbuf, fswap, frecv, obuf, oswap, orecv,
    aloc, ad2d_s, ad2d_r, gloc, gs, gr, ys, yr, ws, wr, h1s, h1r, h2s, h2r, xs, xrs, fss, frs, oss, ors,
    qh, ql, r1, vbuf, qloc, zs, zr, vs, vr, cs, cr, ds, dr,
):
    xh, xl, y, z, c = where()
    me = xh * 8 + z * 2 + c
    mate = device(xh, xl, y, z, 1 - c)
    up, down = device(xh, xl, y + 1, z, c), device(xh, xl, y + 3, z, c)
    fore, back = device(xh, xl, y, z + 1, c), device(xh, xl, y, z + 3, c)
    beside = device(xh, 1 - xl, y, z, c)
    across = device(1 - xh, xl, y, z, c)
    column = [(dz, cc) for cc in range(2) for dz in range(4)][1:]
    peers = [device(xh, xl, y, z + dz, (c + cc) % 2) for dz, cc in column]
    greet(peers + [up, down, beside, across, device(1 - xh, 1 - xl, y, z, c)])

    mine = pl.ds(pl.multiple_of(c * TOK, TOK), TOK)
    own_cols = pl.ds(pl.multiple_of(xl * ROWS, ROWS), ROWS)
    other_cols = pl.ds(pl.multiple_of((1 - xl) * ROWS, ROWS), ROWS)

    def cols(p):
        return pl.ds(pl.multiple_of(p * PW, PW), PW)

    def local_a(p):
        return pltpu.make_async_copy(
            act.at[:, pl.ds(pl.multiple_of(c * BLK + p * PW, PW), PW)], abuf.at[0, mine, cols(p)], aloc.at[p])

    def mate_a(p):
        return remote(
            act.at[:, pl.ds(pl.multiple_of((1 - c) * BLK + p * PW, PW), PW)], abuf.at[0, mine, cols(p)],
            ad2d_s.at[p], ad2d_r.at[p], mate)

    for p in range(NP):
        mate_a(p).start()
        local_a(p).start()
    g_local = pltpu.make_async_copy(og, gbuf.at[mine, own_cols], gloc)
    g_beside = remote(og, gbuf.at[mine, own_cols], gs.at[0], gr.at[0], beside)
    g_mate = remote(og, gbuf.at[mine, own_cols], gs.at[1], gr.at[1], mate)
    g_pass = remote(gbuf.at[mine, other_cols], gbuf.at[mine, other_cols], gs.at[2], gr.at[2], mate)
    g_local.start()
    g_beside.start()
    g_mate.start()

    theirs_too = pl.ds(pl.multiple_of((1 - c) * TOK, TOK), TOK)

    def rounds(p):
        out = []
        for k, rows in enumerate((mine, theirs_too)):
            out.append(remote(
                abuf.at[0, rows, cols(p)], abuf.at[3, rows, cols(p)], ys.at[0, p, k], yr.at[0, p, k], up))
            out.append(remote(
                abuf.at[0, rows, cols(p)], abuf.at[1, rows, cols(p)], ys.at[1, p, k], yr.at[1, p, k], down))
        return tuple(out)

    def relays(p, first, second):
        out = []
        for k in range(RELAYS):
            size = TOK // RELAYS
            low, high = pl.ds(k * size, size), pl.ds(TOK + k * size, size)
            if first:
                out.append(remote(
                    abuf.at[1, low, cols(p)], abuf.at[2, low, cols(p)], ws.at[0, p, k], wr.at[0, p, k], down))
            if second:
                out.append(remote(
                    abuf.at[3, high, cols(p)], abuf.at[2, high, cols(p)], ws.at[1, p, k], wr.at[1, p, k], up))
        return tuple(out)

    for p in range(NP):
        local_a(p).wait()
        if p == 0:
            for copy in rounds(p)[:2]:
                copy.start()
        mate_a(p).wait_recv()
        if p < AHEAD:
            for copy in rounds(p)[2 * (p == 0):]:
                copy.start()

    def factor_rows(p, carry):
        fs[cols(p), :] = contract0(abuf[0, :, cols(p)], abuf[0])
        return carry

    lax.fori_loop(0, NP, factor_rows, 0)
    fbuf[:, 48:64, :] = jnp.zeros((16, 16, BLK), bf16)

    def strips(r, carry):
        fbuf[r, 0:56, :] = fs[pl.ds(pl.multiple_of(r * 56, 8), 56), :].astype(bf16)
        return carry

    lax.fori_loop(0, 16, strips, 0)
    basis = pltpu.make_async_copy(basis_in.at[0], fs, qloc)
    basis.start()
    r1[...] = jnp.zeros_like(r1)
    g_local.wait()
    g_here = gbuf[mine, own_cols]
    obuf[...] = contract0(g_here, g_here).astype(bf16)

    theirs, ours = (1 - xh) * 8, xh * 8
    swap = (
        remote(fbuf.at[pl.ds(theirs, 8)], fswap, fss.at[0], frs.at[0], across),
        remote(obuf.at[pl.ds(pl.multiple_of(theirs * 32, 256), 256), :], oswap, oss.at[0], ors.at[0], across),
    )
    def strip(dz, cc):
        return ((z + dz) % 4) * 2 + (c + cc) % 2

    def send_strip(k):
        dz, cc = column[k - 1]
        to = device(xh, xl, y, z + dz, (c + cc) % 2)
        r = strip(dz, cc)
        return (
            remote(fswap.at[r], frecv.at[k], fss.at[k], frs.at[k], to),
            remote(oswap.at[pl.ds(pl.multiple_of(r * 32, 32), 32), :], orecv.at[k], oss.at[k], ors.at[k], to),
        )

    def send_strips():
        for copy in swap:
            copy.wait_recv()

        def add(r, carry):
            fswap[r] = (fswap[r].astype(f32) + fbuf[ours + r].astype(f32)).astype(bf16)
            return carry

        lax.fori_loop(0, 8, add, 0)
        oswap[...] = (oswap[...].astype(f32)
                      + obuf[pl.ds(pl.multiple_of(ours * 32, 256), 256), :].astype(f32)).astype(bf16)
        for k in range(1, 8):
            for copy in send_strip(k):
                copy.start()

    def partial(d, p, tx):
        e = (y - z + d + 4) % 4
        other = gbuf[:, pl.ds(pl.multiple_of(tx * ROWS, ROWS), ROWS)]
        pbuf[e, tx, cols(p), :] = contract0(abuf[d, :, cols(p)], other).astype(bf16)

    def hop1(p, tx):
        near = pl.ds(pl.multiple_of(p * PW, 64), 64)
        far = pl.ds(pl.multiple_of(p * PW + 64, 64), 64)
        rows = pl.ds(pl.multiple_of(p * 64, 64), 64)
        return (
            remote(pbuf.at[2, tx, near, :], h1.at[0, tx, rows, :], h1s.at[0, p, tx], h1r.at[0, p, tx], fore),
            remote(pbuf.at[2, tx, far, :], h1.at[1, tx, rows, :], h1s.at[1, p, tx], h1r.at[1, p, tx], back),
        )

    def hop2(p, tx):
        return (
            remote(pbuf.at[1, tx, cols(p), :], h2.at[0, tx, cols(p), :], h2s.at[0, p, tx], h2r.at[0, p, tx], fore),
            remote(pbuf.at[3, tx, cols(p), :], h2.at[1, tx, cols(p), :], h2s.at[1, p, tx], h2r.at[1, p, tx], back),
        )

    def add_hop1(p, tx):
        near = pl.ds(pl.multiple_of(p * PW, 64), 64)
        far = pl.ds(pl.multiple_of(p * PW + 64, 64), 64)
        rows = pl.ds(pl.multiple_of(p * 64, 64), 64)
        pbuf[1, tx, near, :] = (pbuf[1, tx, near, :].astype(f32) + h1[0, tx, rows, :].astype(f32)).astype(bf16)
        pbuf[3, tx, far, :] = (pbuf[3, tx, far, :].astype(f32) + h1[1, tx, rows, :].astype(f32)).astype(bf16)

    def to_owner(tx, p):
        return remote(
            sbuf.at[tx, cols(p), :], xr.at[xh, cols(p), :], xs.at[tx, p], xrs.at[xh, p], device(xl, tx, y, z, c))

    def from_half(kx, p):
        return remote(
            sbuf.at[0, cols(p), :], xr.at[kx, cols(p), :], xs.at[0, p], xrs.at[kx, p], beside)

    def is_self(tx):
        return jnp.logical_and(xh == xl, xl == tx)

    def comes_from_self(kx):
        return jnp.logical_and(xh == xl, kx == xh)

    own, oth = xl, 1 - xl

    def product(d, p, tx):
        partial(d, p, tx)

        @pl.when((y - z + d + 4) % 4 == 2)
        def _():
            for copy in hop1(p, tx):
                copy.start()

    def near_tail(p, tx):
        for copy in relays(p, True, True):
            copy.wait_recv()
        product(2, p, tx)

    def step(i, carry):
        @pl.when(i + AHEAD < NP)
        def _():
            for copy in rounds(i):
                copy.wait_send()
            for copy in rounds(i + AHEAD):
                copy.start()

        @pl.when(jnp.logical_and(i >= LAG2, i < NP + LAG2))
        def _():
            p = i - LAG2
            for tx in (own, oth):
                for copy in hop1(p, tx):
                    copy.wait_recv()
                add_hop1(p, tx)
                for copy in hop2(p, tx):
                    copy.start()

        @pl.when(i < NP)
        def _():
            arrivals = rounds(i)
            for k in (1, 3):
                arrivals[k].wait_recv()
            for copy in relays(i, True, False):
                copy.start()
            for k in (0, 2):
                arrivals[k].wait_recv()
            for copy in relays(i, False, True):
                copy.start()

            @pl.when(i == 0)
            def _():
                g_mate.wait_recv()

            for d in (0, 1, 3):
                product(d, i, own)

            @pl.when(i == 1)
            def _():
                g_pass.wait_recv()
                for d in (0, 1, 3):
                    product(d, 0, oth)

            @pl.when(i >= 1)
            def _():
                for d in (0, 1, 3):
                    product(d, i, oth)

            @pl.when(i == 0)
            def _():
                g_beside.wait_recv()
                g_pass.start()
                for copy in swap:
                    copy.start()
                near_tail(0, own)

        @pl.when(jnp.logical_and(i >= 1, i < NP + 1))
        def _():
            p = i - 1

            @pl.when(i > 1)
            def _():
                near_tail(p, own)

            product(2, p, oth)

        @pl.when(jnp.logical_and(i >= LAG3, i < NP + LAG3))
        def _():
            p = i - LAG3
            for tx in range(2):
                for copy in hop2(p, tx):
                    copy.wait_recv()
                total = (pbuf[0, tx, cols(p), :].astype(f32) + h2[0, tx, cols(p), :].astype(f32)
                         + h2[1, tx, cols(p), :].astype(f32))
                sbuf[tx, cols(p), :] = total.astype(bf16)

                @pl.when(is_self(tx))
                def _():
                    xr[xh, cols(p), :] = total.astype(bf16)

                @pl.when(jnp.logical_not(is_self(tx)))
                def _():
                    to_owner(tx, p).start()

        @pl.when(i == 2)
        def _():
            basis.wait()

            def halves(p, carry):
                high, low = split(fs[cols(p), :])
                qh[cols(p), :] = high
                ql[cols(p), :] = low
                return carry

            lax.fori_loop(0, NP, halves, 0)

        @pl.when(i == STRIPS)
        def _():
            send_strips()

        @pl.when(i >= LAG4)
        def _():
            p = i - LAG4
            for kx in range(2):
                @pl.when(jnp.logical_not(comes_from_self(kx)))
                def _():
                    from_half(kx, p).wait_recv()
            high, low = split((xr[0, cols(p), :].astype(f32) + xr[1, cols(p), :].astype(f32)) * SCALE)
            left = jnp.concatenate([qh[cols(p), :], ql[cols(p), :], qh[cols(p), :]], axis=0)
            right = jnp.concatenate([high, high, low], axis=0)
            r1[...] += contract0(left, right)

        return carry

    lax.fori_loop(0, NP + LAG4, step, 0)

    oh, ol = split(basis_out[...])
    for start, size in (FIRST, LAST):
        rows = slice(start, start + size)
        mh, ml = split(r1[rows, :])
        turned = dot(mh, oh) + dot(mh, ol) + dot(ml, oh)
        for p in range(start // 128, (start + size) // 128):
            spread = jnp.transpose(jnp.broadcast_to(eigen_in[p : p + 1, :], (128, 128)))
            for k in range(ROWS // 128):
                lanes = slice(k * 128, (k + 1) * 128)
                scaled = turned[p * 128 - start : (p + 1) * 128 - start, lanes] / (
                    spread * eigen_out[:, lanes] + damping)
                vbuf[p * 128 : (p + 1) * 128, lanes] = scaled.astype(bf16)
        back_out = lax.dot_general(
            vbuf[rows, :], oh, (((1,), (1,)), ((), ())), preferred_element_type=f32)
        vbuf[rows, :] = back_out.astype(bf16)

    def part(other, dz, core, start, size):
        half = (1 - xh) if other else xh
        base = (half * 8 + ((z + dz) % 4) * 2 + core) * BLK
        return u.at[pl.ds(pl.multiple_of(base + start, 64), size), :]

    def hand(other, dz, start, size, ssem, rsem, to):
        return remote(part(other, dz, c, start, size), part(other, dz, c, start, size), ssem, rsem, to)

    waits = []

    def go(descriptor):
        descriptor.start()
        waits.append(descriptor)
        return descriptor

    def ring(sem, other, start, size):
        go(hand(other, 0, start, size, zs.at[0, sem], zr.at[0, sem], fore))
        go(hand(other, 0, start, size, zs.at[1, sem], zr.at[1, sem], back))

    def ring_take(sem, other, start, size):
        hand(other, 3, start, size, zs.at[0, sem], zr.at[0, sem], fore).wait_recv()
        hand(other, 1, start, size, zs.at[1, sem], zr.at[1, sem], back).wait_recv()

    def relay(sem, other, start, size):
        half = size // 2
        go(hand(other, 3, start, half, vs.at[0, sem], vr.at[0, sem], fore))
        go(hand(other, 1, start + half, half, vs.at[1, sem], vr.at[1, sem], back))

    def relay_take(sem, other, start, size):
        half = size // 2
        hand(other, 2, start, half, vs.at[0, sem], vr.at[0, sem], fore).wait_recv()
        hand(other, 2, start + half, half, vs.at[1, sem], vr.at[1, sem], back).wait_recv()

    def cross(sem, dz, start, size):
        go(hand(False, dz, start, size, cs.at[sem], cr.at[sem], across))

    def cross_take(sem, dz, start, size):
        hand(True, dz, start, size, cs.at[sem], cr.at[sem], across).wait_recv()

    given = []

    def share(other, dz, start, size):
        sem = len(given)
        go(hand(other, dz, start, size, ds.at[sem], dr.at[sem], mate))
        given.append((other, dz, start, size))

    for k, (start, size) in enumerate(PARTS):
        block = dot(qh[start : start + size, :], vbuf[...]).astype(bf16)
        u[pl.ds(pl.multiple_of(me * BLK + start, 64), size), :] = block
        if k < 2:
            cross(k, 0, start, size)
            ring(k, False, start, size)
        if k == 3:
            ring(2, False, *LAST)
            cross(2, 0, *LAST)
    share(False, 0, *FIRST)
    share(False, 0, *LAST)
    for k in range(2):
        ring_take(k, False, *PARTS[k])
        relay(k, False, *PARTS[k])
    for k in range(2):
        cross_take(k, 0, *PARTS[k])
        ring(3 + k, True, *PARTS[k])
    ring_take(2, False, *LAST)
    relay(2, False, *LAST)
    cross(3, 1, *LAST)
    cross(4, 3, *LAST)
    for dz in (1, 3):
        share(False, dz, 0, BLK)
    share(True, 0, *FIRST)
    for k in range(2):
        relay_take(k, False, *PARTS[k])
    share(False, 2, *FIRST)
    relay_take(2, False, *LAST)
    cross(5, 2, *LAST)
    share(False, 2, *LAST)
    cross_take(2, 0, *LAST)
    share(True, 0, *LAST)
    for k in range(2):
        ring_take(3 + k, True, *PARTS[k])
        relay(3 + k, True, *PARTS[k])
    share(True, 1, *FIRST)
    share(True, 3, *FIRST)
    cross_take(3, 1, *LAST)
    share(True, 1, *LAST)
    cross_take(4, 3, *LAST)
    share(True, 3, *LAST)
    cross_take(5, 2, *LAST)
    share(True, 2, *LAST)
    for k in range(2):
        relay_take(3 + k, True, *PARTS[k])
        share(True, 2, *PARTS[k])
    for k in range(1, 8):
        for copy in send_strip(k):
            copy.wait_recv()
    here = fswap[z * 2 + c, 0:56, :].astype(f32)
    for k in range(1, 4):
        here += frecv[k, 0:56, :].astype(f32)
    there = frecv[4, 0:56, :].astype(f32)
    for k in range(5, 8):
        there += frecv[k, 0:56, :].astype(f32)
    fin_out[c] = here * SCALE
    fin_out[1 - c] = there * SCALE
    total = oswap[pl.ds(pl.multiple_of((z * 2 + c) * 32, 32), 32), :].astype(f32)
    for k in range(1, 8):
        total += orecv[k].astype(f32)
    fout_out[...] = total * SCALE

    for sem, (other, dz, start, size) in enumerate(given):
        ref = part(other, dz, 1 - c, start, size)
        remote(ref, ref, ds.at[sem], dr.at[sem], mate).wait_recv()
    for descriptor in waits:
        descriptor.wait_send()

    for copy in (g_beside, g_mate, g_pass):
        copy.wait_send()

    def finish(p, carry):
        mate_a(p).wait_send()
        for copy in relays(p, True, True):
            copy.wait_send()
        for tx in range(2):
            for copy in hop1(p, tx) + hop2(p, tx):
                copy.wait_send()

            @pl.when(jnp.logical_not(is_self(tx)))
            def _():
                to_owner(tx, p).wait_send()
        return carry

    lax.fori_loop(0, NP, finish, 0)
    for p in range(NP - AHEAD, NP):
        for copy in rounds(p):
            copy.wait_send()

    for copy in swap:
        copy.wait_send()
    for k in range(1, 8):
        for copy in send_strip(k):
            copy.wait_send()


def whole_step(activations, output_grads, basis_in, eigen_in, basis_out, eigen_out):
    dma = pltpu.SemaphoreType.DMA
    any_spec = pl.BlockSpec(memory_space=pl.ANY)
    vmem = pl.BlockSpec(memory_space=pltpu.VMEM)
    return pl.pallas_call(
        step_kernel,
        out_shape=(
            pltpu.VMEM((16 * BLK, ROWS), bf16),
            jax.ShapeDtypeStruct((2, 56, BLK), f32),
            jax.ShapeDtypeStruct((32, ROWS), f32),
        ),
        in_specs=[any_spec, any_spec, any_spec, vmem, vmem, vmem],
        out_specs=(vmem, vmem, vmem),
        scratch_shapes=[
            pltpu.VMEM((4, 2 * TOK, BLK), bf16),
            pltpu.VMEM((2 * TOK, 2 * ROWS), bf16),
            pltpu.VMEM((4, 2, BLK, ROWS), bf16),
            pltpu.VMEM((2, 2, BLK // 2, ROWS), bf16),
            pltpu.VMEM((2, 2, BLK, ROWS), bf16),
            pltpu.VMEM((2, BLK, ROWS), bf16),
            pltpu.VMEM((2, BLK, ROWS), bf16),
            pltpu.VMEM((BLK, BLK), f32),
            pltpu.VMEM((16, 64, BLK), bf16),
            pltpu.VMEM((8, 64, BLK), bf16),
            pltpu.VMEM((8, 64, BLK), bf16),
            pltpu.VMEM((ROWS, ROWS), bf16),
            pltpu.VMEM((ROWS // 2, ROWS), bf16),
            pltpu.VMEM((8, 32, ROWS), bf16),
            dma((NP,)), dma((NP,)), dma((NP,)),
            dma, dma((3,)), dma((3,)),
            dma((2, NP, 2)), dma((2, NP, 2)), dma((2, NP, RELAYS)), dma((2, NP, RELAYS)),
            dma((2, NP, 2)), dma((2, NP, 2)), dma((2, NP, 2)), dma((2, NP, 2)),
            dma((2, NP)), dma((2, NP)),
            dma((8,)), dma((8,)), dma((8,)), dma((8,)),
            pltpu.VMEM((BLK, BLK), bf16),
            pltpu.VMEM((BLK, BLK), bf16),
            pltpu.VMEM((BLK, ROWS), f32),
            pltpu.VMEM((BLK, ROWS), bf16),
            dma,
            dma((2, 5)), dma((2, 5)), dma((2, 5)), dma((2, 5)),
            dma((6,)), dma((6,)), dma((20,)), dma((20,)),
        ],
        compiler_params=pltpu.CompilerParams(
            collective_id=0, has_side_effects=True, vmem_limit_bytes=48 * 2**20),
        cost_estimate=pl.CostEstimate(flops=15_000_000_000, bytes_accessed=26_000_000, transcendentals=0),
        name="kfac_step",
    )(activations, output_grads, basis_in, eigen_in, basis_out, eigen_out)


def body(activations, output_grads, basis_in, eigen_in, basis_out, eigen_out):
    update, fin, factor_out = whole_step(
        activations, output_grads, basis_in, eigen_in.reshape(NP, PW), basis_out, eigen_out.reshape(1, ROWS))
    return (update, jnp.transpose(fin, (1, 0, 2)), factor_out)


def solution(mesh):
    in_specs = (
        P("dp", "tensor"),
        P("dp", "tensor"),
        P("dp", None, None),
        P("dp"),
        P("tensor", None),
        P("tensor"),
    )
    out_specs = (P(None, "tensor"), P("dp", "tensor", None), P("dp", "tensor"))
    return jax.shard_map(body, mesh=mesh, in_specs=in_specs, out_specs=out_specs, check_vma=False)
```
